256 devices in a mesh: ctx: 64 (over z_lo, y, x), head: 4 (over z_hi, core).
Axes of the slice: x: 4, y: 4, z: 8 (z_hi: 2, z_lo: 4; z = z_hi * 4 + z_lo), core: 2. Of those that a mesh axis runs over, the one named last changes fastest.
Arguments:
- queries: bfloat16 [16384, 8192], P(('ctx', 'head')), may hold values from -9 to 9
- keys: bfloat16 [16384, 512], P('ctx', 'head'), may hold values from -9 to 9
- values: bfloat16 [16384, 512], P('ctx', 'head'), may hold values from -6 to 6
- doc_lengths: int32 [8], replicated, may hold values from 1 to 8192, 16384 in all
Outputs:
- attended: bfloat16 [16384, 8192], P(('ctx', 'head'))
The draws below stay inside these ranges and needn't reach their ends.
Inputs may be any that keep to these rules, and one draw needn't show every extreme that they name: `doc_lengths`: the lengths sum to 16384 and the largest is exactly 8192.
All inputs are finite; a program needn't handle non-finite values.
Results may differ from the reference program's by a relative error of at most 0.0055.
Values may be sent and summed in bfloat16 or wider, within the bound.
A program may use at most 64 MiB of HBM per device.

```python
import math
import jax
import jax.numpy as jnp
import numpy as np
from jax import lax

HD = 128
GROUP = 16
NDOCS = 8
KVH = 4
QH = 64
SEQ = 16384
MAXDOC = 8192


def draw_queries(key, part):
    key = jax.random.fold_in(key, 1)
    result = jnp.clip(jax.random.normal(key, (SEQ, QH * HD), jnp.float32), -6.0, 6.0)
    return result.astype(jnp.bfloat16)


def draw_keys(key, part):
    key = jax.random.fold_in(key, 2)
    result = jnp.clip(jax.random.normal(key, (SEQ, KVH * HD), jnp.float32), -6.0, 6.0)
    return result.astype(jnp.bfloat16)


def levels(rng, dims, shards, low, top_value):
    loudness = 1.0
    for axis_at, blocks in shards:
        draws = jax.random.uniform(jax.random.fold_in(jax.random.fold_in(rng, 6), axis_at), (blocks,), jnp.float32, low / len(shards), top_value / len(shards))
        loudness = loudness * jnp.repeat(jnp.exp(draws), dims[axis_at] // blocks).reshape((-1,) + (1,) * (len(dims) - 1 - axis_at))
    return loudness


def length_profile(amount, total, most, slope):
    loads = [(1 << 20) // math.isqrt(grade ** slope) + 1 for grade in range(2, amount + 1)]
    surplus, holding = total - most - (amount - 1), [1] * (amount - 1)
    while surplus > 0:
        candidates = [i for i in range(amount - 1) if holding[i] < most]
        whole, left = sum([loads[i] for i in candidates]), surplus
        for i in candidates:
            more = min(most - holding[i], max(1, left * loads[i] // whole), surplus)
            holding[i] = holding[i] + more
            surplus = surplus - more
    return np.array([most] + holding)


def uneven(rng, count, total, reach, skew):
    if count == 2:
        one = jax.random.randint(rng, (), max(1, total - reach), min(reach, total - 1) + 1)
        return jnp.stack([one, total - one])
    lengths = jnp.asarray(length_profile(count, total, reach, skew), jnp.int32)
    couples = (count - 1) // 2
    giver, taker = lengths[1:1 + 2 * couples:2], lengths[2:2 + 2 * couples:2]
    slack = jnp.minimum(giver - 1, reach - taker)
    shifted = jax.random.randint(jax.random.fold_in(rng, 1), (couples,), 0, 1 << 20) % (slack + 1)
    lengths = lengths.at[1:1 + 2 * couples:2].set(giver - shifted).at[2:2 + 2 * couples:2].set(taker + shifted)
    return lengths[jax.random.permutation(jax.random.fold_in(rng, 2), count)]


def noise(own_key, extent, width, reach, cuts=(), kind=jnp.bfloat16):
    gain = levels(own_key, extent, cuts, -0.22, 0.18) if cuts else 1.0
    values = jax.random.normal(own_key, extent, jnp.float32) * width * gain
    return jnp.minimum(jnp.maximum(values, -reach), reach).astype(kind)


def setup_inputs(seed: int = 0) -> dict:
    arg_keys = jax.random.split(jax.random.key(seed), 5)
    queries = draw_queries(jax.random.fold_in(arg_keys[4], 71), 0)
    keys = draw_keys(jax.random.fold_in(arg_keys[4], 71), 0)
    values = noise(arg_keys[2], (SEQ, KVH * HD), 1.0, 6.0, ((0, 64), (1, 4)))
    doc_lengths = uneven(arg_keys[3], NDOCS, SEQ, MAXDOC, 2).astype(jnp.int32)
    return {"queries": queries, "keys": keys, "values": values, "doc_lengths": doc_lengths}


neg_big = -1e+30

def reference(queries, keys, values, doc_lengths):
    seq_len = queries.shape[0]
    heads_kv = keys.shape[1] // HD
    tile_rows = 256
    block_rows = 256
    score_scale = 1.0 / math.sqrt(HD)
    doc_starts = (jnp.cumsum(doc_lengths) - doc_lengths).astype(jnp.int32)
    grouped_q = queries.reshape(seq_len // tile_rows, tile_rows, heads_kv, GROUP, HD)
    keys_3d = keys.reshape(seq_len, heads_kv, HD)
    values_3d = values.reshape(seq_len, heads_kv, HD)

    def one_tile(tile_index):
        tile_start = (tile_index * tile_rows).astype(jnp.int32)
        q_tile = lax.dynamic_index_in_dim(grouped_q, tile_index, 0, keepdims=False).astype(jnp.float32)
        positions = tile_start + jnp.arange(tile_rows, dtype=jnp.int32)
        hit = doc_starts[None, :] <= positions[:, None]
        begins = lax.optimization_barrier(jnp.max(jnp.where(hit, doc_starts[None, :], 0), axis=1)).astype(jnp.int32)
        first_block = (begins[0] // block_rows).astype(jnp.int32)
        last_block = ((tile_start + tile_rows - 1) // block_rows + 1).astype(jnp.int32)

        def block_scores(block_index):
            offset = (block_index * block_rows).astype(jnp.int32)
            key_block = lax.dynamic_slice_in_dim(keys_3d, offset, block_rows, 0).astype(jnp.float32)
            scores = jnp.einsum('tkgd,skd->tkgs', q_tile, key_block) * score_scale
            key_pos = offset + jnp.arange(block_rows, dtype=jnp.int32)
            visible = (key_pos[None, :] <= positions[:, None]) & (key_pos[None, :] >= begins[:, None])
            return (scores, visible[:, None, None, :], offset)

        def find_top(block_index, top_score):
            scores, visible, offset = block_scores(block_index)
            return jnp.maximum(top_score, lax.optimization_barrier(jnp.max(jnp.where(visible, scores, neg_big), axis=3)))
        top_score = lax.fori_loop(first_block, last_block, find_top, jnp.full((tile_rows, heads_kv, GROUP), neg_big, jnp.float32))

        def add_block(block_index, carried):
            denominator, running = carried
            scores, visible, offset = block_scores(block_index)
            weights = jnp.where(visible, jnp.exp(scores - top_score[..., None]), 0.0)
            value_block = lax.dynamic_slice_in_dim(values_3d, offset, block_rows, 0).astype(jnp.float32)
            rounded = weights.astype(jnp.bfloat16).astype(jnp.float32)
            denominator = denominator + lax.optimization_barrier(jnp.sum(weights, axis=3))
            running = running + jnp.einsum('tkgs,skd->tkgd', rounded, value_block)
            return (denominator, running)
        denominator, running = lax.fori_loop(first_block, last_block, add_block, (jnp.zeros((tile_rows, heads_kv, GROUP), jnp.float32), jnp.zeros((tile_rows, heads_kv, GROUP, HD), jnp.float32)))
        result = (running / denominator[..., None]).astype(jnp.bfloat16)
        return result.reshape(tile_rows, heads_kv * GROUP * HD)
    tiles_out = lax.map(one_tile, jnp.arange(seq_len // tile_rows, dtype=jnp.int32))
    return tiles_out.reshape(seq_len, heads_kv * GROUP * HD)
```

```python
import math

import jax
import jax.numpy as jnp
from jax import lax
from jax.experimental import pallas as pl
from jax.experimental.pallas import tpu as pltpu
from jax.sharding import PartitionSpec as P

neg_big = -1e30
block_keys = 512
MESH = pl.DeviceIdType.MESH

head_depth = 128
heads_per_group = 16
group_columns = heads_per_group * head_depth
own_tokens = 64
block = 256
row_keys = 4 * block
slot_columns = own_tokens * heads_per_group
exponent_scale = math.log2(math.e) / math.sqrt(head_depth)
safe_exponent = 100.0


def attend_kernel(
    q_ref,
    k_ref,
    v_ref,
    len_ref,
    out_ref,
    stat_ref,
    stage,
    keyval,
    q_in,
    q_cols,
    acc,
    denom,
    begins,
    o_part,
    stat_own,
    stat_in,
    stage_sem,
    row_sem,
    q_sem,
    o_sem,
    stat_sem,
    z_send,
    plane_send,
    q_send,
    sib_send,
    o_send,
    stat_send,
):
    ctx = lax.axis_index("ctx")
    head = lax.axis_index("head")
    plane, y, x = ctx // 16, (ctx // 4) % 4, ctx % 4
    half, core = head // 2, head % 2
    ybit, xbit, yhi = y % 2, x % 2, y // 2
    group = ybit * 2 + xbit
    quad_row = plane * 4 + yhi * 2
    receiver = core == xbit

    def ctx_of(p, yy, xx):
        return p * 16 + yy * 4 + xx

    barrier = pltpu.get_barrier_semaphore()
    partners = []
    for dy in range(4):
        for dx in range(4):
            if dy or dx:
                partners.append((ctx_of(plane, (y + dy) % 4, (x + dx) % 4), head))
    for dz in range(1, 8):
        z = (half * 4 + plane + dz) % 8
        partners.append((ctx_of(z % 4, y, x), (z // 4) * 2 + core))
    sibling = (ctx, half * 2 + 1 - core)
    partners.append(sibling)
    for partner in partners:
        pl.semaphore_signal(barrier, inc=1, device_id=partner, device_id_type=MESH)

    mine = half * 4 + plane
    stage[mine, 0] = k_ref[...]
    v_t = v_ref[...].T
    stage[mine, 1] = jnp.concatenate([v_t[:, :128], v_t[:, 128:]], axis=0)
    pl.semaphore_wait(barrier, len(partners))

    def remote(src, dst, send, recv, target):
        return pltpu.make_async_remote_copy(
            src_ref=src,
            dst_ref=dst,
            send_sem=send,
            recv_sem=recv,
            device_id=target,
            device_id_type=MESH,
        )

    def z_copy(n, flip, ahead):
        to_half = (half + flip) % 2
        return remote(
            stage.at[mine],
            stage.at[mine],
            z_send.at[n],
            stage_sem.at[mine],
            (ctx_of(plane + ahead, y, x), to_half * 2 + core),
        )

    z_plan = [(1, 0), (0, 1), (1, 1), (0, 2), (1, 2)]
    for n, (flip, ahead) in enumerate(z_plan):
        pl.when(plane + ahead < 4)(lambda n=n, f=flip, a=ahead: z_copy(n, f, a).start())

    def plane_copies(flip, back, act):
        g = (half + flip) % 2
        p = plane - back
        index = g * 4 + p
        n = flip * 3 + back
        for to_yhi in range(2):
            for to_xhi in range(2):
                to_y, to_x = to_yhi * 2 + g, to_xhi * 2 + core
                wanted = p >= 0
                if back == 0:
                    wanted &= yhi <= to_yhi
                if back == 2:
                    wanted &= yhi >= to_yhi
                here = (to_y == y) & (to_x == x)
                row = p * 4 + y
                sem = plane_send.at[n * 4 + to_yhi * 2 + to_xhi]

                @pl.when(wanted & jnp.logical_not(here))
                def _():
                    copy = remote(
                        stage.at[index],
                        keyval.at[row, :, x],
                        sem,
                        row_sem.at[row],
                        (ctx_of(plane, to_y, to_x), head),
                    )
                    copy.start() if act == "start" else copy.wait_send()

                if act == "start":

                    @pl.when(wanted & here)
                    def _():
                        pltpu.make_async_copy(
                            stage.at[index], keyval.at[row, :, x], row_sem.at[row]
                        ).start()

    def mate(k):
        my, mx = (ybit + k // 2) % 2, (xbit + k % 2) % 2
        return my, mx

    def q_copy(k):
        my, mx = mate(k)
        columns = pl.ds(pl.multiple_of((my * 2 + mx) * group_columns, 128), group_columns)
        return remote(
            q_ref.at[:, columns],
            q_in.at[group],
            q_send.at[k],
            q_sem.at[group],
            (ctx_of(plane, yhi * 2 + my, (x // 2) * 2 + mx), head),
        )

    def slot_copy(k):
        my, mx = mate(k)
        slot = my * 2 + mx
        return remote(q_in.at[slot], q_in.at[slot], q_send.at[0], q_sem.at[slot], sibling)

    plane_copies(0, 0, "start")
    for k in (1, 2, 3):
        q_copy(k).start()

    def relay(flip, back):
        @pl.when(plane >= back)
        def _():
            index = ((half + flip) % 2) * 4 + plane - back
            remote(
                stage.at[index], stage.at[index], z_send.at[5], stage_sem.at[index], sibling
            ).wait_recv()

        plane_copies(flip, back, "start")

    lane = lax.broadcasted_iota(jnp.int32, (8, 128), 1) % own_tokens
    starts = []
    total = jnp.int32(0)
    for d in range(8):
        starts.append(total)
        total = total + len_ref[d]

    def slot_position(slot):
        c = ctx_of(plane, yhi * 2 + slot // 2, (x // 2) * 2 + slot % 2)
        return c * block + head * own_tokens

    for slot in range(4):
        position = slot_position(slot) + lane
        begin = jnp.zeros((8, 128), jnp.int32)
        for start in starts:
            begin = jnp.maximum(begin, jnp.where(position >= start, start, 0))
        begins[slot] = begin

    acc[...] = jnp.zeros_like(acc)
    denom[...] = jnp.zeros_like(denom)
    own_keys = k_ref[...].astype(jnp.float32)
    key_norm = jnp.max(jnp.sum(own_keys * own_keys, axis=1))

    def columns_of(slot, read):
        best = jnp.zeros((1, 128), jnp.float32)
        for pair in range(8):
            two = read(pair)
            tile = jnp.concatenate([two[:, :128], two[:, 128:]], axis=0)
            turned = tile.astype(jnp.float32).T
            best = jnp.maximum(best, jnp.sum(turned * turned, axis=0, keepdims=True))
            at = pl.multiple_of(slot * slot_columns + pair * 128, 128)
            q_cols[:, pl.ds(at, 128)] = turned.astype(jnp.bfloat16)
        return best

    def read_own(pair):
        at = pl.multiple_of(group * group_columns + pair * 256, 128)
        return q_ref[:, pl.ds(at, 256)]

    query_norm = columns_of(group, read_own)

    relay(1, 0)
    relay(0, 1)
    relay(1, 1)

    for k in (1, 2, 3):
        slot_copy(k).wait_recv()
        my, mx = mate(k)
        slot = my * 2 + mx
        query_norm = jnp.maximum(
            query_norm,
            columns_of(slot, lambda pair, s=slot: q_in[s, :, pl.ds(pair * 256, 256)]),
        )

    rank = lax.broadcasted_iota(jnp.int32, (8, 128), 0)
    stat_own[0] = jnp.where(rank < 4, jnp.broadcast_to(query_norm, (8, 128)), key_norm)

    rounds = [[(0, sibling)], [], [], []]
    for d in range(1, 4):
        rounds[1].append((d, (ctx_of(plane, y, (x + d) % 4), head)))
        rounds[2].append((3 + d, (ctx_of(plane, (y + d) % 4, x), head)))
    for dz in range(1, 8):
        z = (half * 4 + plane + dz) % 8
        rounds[3].append((6 + dz, (ctx_of(z % 4, y, x), (z // 4) * 2 + core)))

    def stat_copy(r, n, target):
        return remote(stat_own.at[r], stat_in.at[n], stat_send.at[n], stat_sem.at[n], target)

    def stat_start(r):
        for n, target in rounds[r]:
            stat_copy(r, n, target).start()

    def stat_finish(r):
        best = stat_own[r]
        for n, target in rounds[r]:
            stat_copy(r, n, target).wait()
            best = jnp.maximum(best, stat_in[n])
        stat_own[r + 1] = best

    def sib_copy(row):
        return remote(keyval.at[row], keyval.at[row], sib_send.at[row], row_sem.at[row], sibling)

    def take_row(row):
        @pl.when(row >= 0)
        def _():
            sib_copy(row).wait_recv()

            @pl.when(receiver)
            def _():
                sib_copy(row).start()

    key_rank = lax.broadcasted_iota(jnp.int32, (block, 128), 0)

    def absorb_keys(slot, keys, values_t, masks):
        columns = pl.ds(pl.multiple_of(slot * slot_columns, 128), slot_columns)
        scores = jnp.dot(keys, q_cols[:, columns], preferred_element_type=jnp.float32)
        visible = jnp.concatenate(masks, axis=0)
        visible = jnp.concatenate([visible] * (slot_columns // 128), axis=1)
        weights = jnp.where(visible, jnp.exp2(scores * exponent_scale), 0.0)
        denom[:, columns] += jnp.sum(weights.reshape(-1, 8, slot_columns), axis=0)
        acc[:, columns] += jnp.dot(
            values_t, weights.astype(jnp.bfloat16), preferred_element_type=jnp.float32
        )

    def turned_values(tile):
        return jnp.concatenate([tile[:128], tile[128:]], axis=1)

    def full_row(row, slot):
        begin = begins[slot][:1]
        absorb_keys(
            slot,
            keyval[row, 0].reshape(row_keys, head_depth),
            jnp.concatenate([turned_values(keyval[row, 1, i]) for i in range(4)], axis=1),
            [key_rank + (row * row_keys + i * block) >= begin for i in range(4)],
        )

    def edge_rows(slot):
        slot_y, slot_x = yhi * 2 + slot // 2, (x // 2) * 2 + slot % 2
        near = plane * 4 + slot_y
        far = near - 8
        held = jnp.maximum(far, 0) * (far >= 0).astype(jnp.int32) + near * (far < 0).astype(jnp.int32)
        begin = begins[slot][:1]
        position = slot_position(slot) + lane[:1]
        keys, values_t, masks = [], [], []
        for i in range(4):
            is_near = (slot_x >= i).astype(jnp.int32)
            row = is_near * near + (1 - is_near) * held
            first = (is_near * near + (1 - is_near) * far) * row_keys + i * block
            keys.append(keyval[row, 0, i])
            values_t.append(turned_values(keyval[row, 1, i]))
            key = key_rank + first
            masks.append((key >= begin) & (key <= position))
        absorb_keys(slot, jnp.concatenate(keys, axis=0), jnp.concatenate(values_t, axis=1), masks)

        @pl.when(far >= 0)
        def _():
            first = far * row_keys + slot_x * block
            absorb_keys(
                slot,
                keyval[held, 0, slot_x],
                turned_values(keyval[held, 1, slot_x]),
                [key_rank + first >= begin],
            )

    take_row(quad_row)

    @pl.loop(2, 4)
    def _(slot):
        full_row(quad_row, slot)

    stat_start(0)
    take_row(quad_row + 1)
    relay(0, 2)
    relay(1, 2)
    for t in range(1, 7):
        row = quad_row - t
        take_row(row)

        @pl.when(row >= 0)
        def _():
            @pl.loop(0, 4)
            def _(slot):
                full_row(row, slot)

        if t <= 4:
            stat_finish(t - 1)
            if t < 4:
                stat_start(t)
    stat_ref[...] = stat_own[4]
    take_row(quad_row - 7)
    take_row(quad_row - 8)

    def o_copy(k):
        my, mx = mate(k)
        columns = pl.ds(pl.multiple_of(group * group_columns, 128), group_columns)
        return remote(
            o_part.at[my * 2 + mx],
            out_ref.at[:, columns],
            o_send.at[k],
            o_sem.at[k],
            (ctx_of(plane, yhi * 2 + my, (x // 2) * 2 + mx), head),
        )

    for k in (3, 2, 1, 0):
        my, mx = mate(k)
        slot = my * 2 + mx

        @pl.when((my == 0) & (quad_row >= 7))
        def _():
            full_row(quad_row - 7, slot)

        edge_rows(slot)

        for pair in range(8):
            columns = pl.ds(pl.multiple_of(slot * slot_columns + pair * 128, 128), 128)
            share = acc[:, columns] / jnp.sum(denom[:, columns], axis=0, keepdims=True)
            back = share.T.astype(jnp.bfloat16)
            if k:
                o_part[slot, :, pl.ds(pair * 256, 128)] = back[:own_tokens]
                o_part[slot, :, pl.ds(pair * 256 + 128, 128)] = back[own_tokens:]
            else:
                at = pl.multiple_of(group * group_columns + pair * 256, 128)
                out_ref[:, pl.ds(at, 128)] = back[:own_tokens]
                out_ref[:, pl.ds(pl.multiple_of(at + 128, 128), 128)] = back[own_tokens:]
        if k:
            o_copy(k).start()

    for k in (1, 2, 3):
        q_copy(k).wait_send()
    for n, (flip, ahead) in enumerate(z_plan):
        pl.when(plane + ahead < 4)(lambda n=n, f=flip, a=ahead: z_copy(n, f, a).wait_send())
    for flip in range(2):
        for back in range(3):
            plane_copies(flip, back, "wait")
    for t in range(-1, 9):
        row = quad_row - t

        @pl.when((row >= 0) & receiver)
        def _():
            sib_copy(row).wait_send()

    for k in (3, 2, 1):
        o_copy(k).wait()


def attend(queries, keys, values, doc_lengths):
    vmem = pl.BlockSpec(memory_space=pltpu.VMEM)
    smem = pl.BlockSpec(memory_space=pltpu.SMEM)
    elements = 9 * row_keys * 4 * slot_columns
    dma = pltpu.SemaphoreType.DMA
    return pl.pallas_call(
        attend_kernel,
        name="attend",
        out_shape=(
            jax.ShapeDtypeStruct(queries.shape, jnp.bfloat16),
            jax.ShapeDtypeStruct((8, 128), jnp.float32),
        ),
        in_specs=[vmem, vmem, vmem, smem],
        out_specs=(vmem, vmem),
        scratch_shapes=[
            pltpu.VMEM((8, 2, block, head_depth), jnp.bfloat16),
            pltpu.VMEM((16, 2, 4, block, head_depth), jnp.bfloat16),
            pltpu.VMEM((4, own_tokens, group_columns), jnp.bfloat16),
            pltpu.VMEM((head_depth, 4 * slot_columns), jnp.bfloat16),
            pltpu.VMEM((head_depth, 4 * slot_columns), jnp.float32),
            pltpu.VMEM((8, 4 * slot_columns), jnp.float32),
            pltpu.VMEM((4, 8, 128), jnp.int32),
            pltpu.VMEM((4, own_tokens, group_columns), jnp.bfloat16),
            pltpu.VMEM((5, 8, 128), jnp.float32),
            pltpu.VMEM((14, 8, 128), jnp.float32),
            dma((8,)),
            dma((16,)),
            dma((4,)),
            dma((4,)),
            dma((14,)),
            dma((6,)),
            dma((24,)),
            dma((4,)),
            dma((16,)),
            dma((4,)),
            dma((14,)),
        ],
        compiler_params=pltpu.CompilerParams(
            collective_id=0, has_side_effects=True, vmem_limit_bytes=56 << 20
        ),
        cost_estimate=pl.CostEstimate(
            flops=4 * elements * head_depth, bytes_accessed=4 << 20, transcendentals=elements
        ),
    )(queries, keys, values, doc_lengths)
def token_begins(doc_starts, positions):
    hit = doc_starts[None, :] <= positions[:, None]
    return jnp.max(jnp.where(hit, doc_starts[None, :], 0), axis=1)


def absorb(
    carried, held_tiles, tile_starts, doc_starts, key_piece, value_piece, piece_start, tok_rows
):
    top_scores, denominators, runnings = carried
    piece_rows = key_piece.shape[0]
    block_width = math.gcd(piece_rows, block_keys)
    tile_count, query_rows, head_depth = held_tiles.shape
    group_size = query_rows // tok_rows
    score_scale = 1.0 / math.sqrt(head_depth)
    new_tops, new_denoms, new_runs = ([], [], [])
    for tile_num in range(tile_count):
        tile_start = tile_starts[tile_num]
        positions = tile_start + jnp.arange(tok_rows, dtype=jnp.int32)
        begins = token_begins(doc_starts, positions)
        low_pos = jnp.maximum(begins[0], piece_start)
        high_pos = jnp.minimum(tile_start + tok_rows, piece_start + piece_rows)
        first_block = low_pos // block_width
        last_block = jnp.maximum(first_block, (high_pos + block_width - 1) // block_width)
        tile_query = held_tiles[tile_num]

        def add_block(block_index, loop_state):
            top_score, denominator, running = loop_state
            offset = block_index * block_width
            key_block = lax.dynamic_slice_in_dim(key_piece, offset, block_width, 0)
            value_block = lax.dynamic_slice_in_dim(value_piece, offset, block_width, 0)
            scores = (
                lax.dot_general(
                    tile_query,
                    key_block,
                    (((1,), (1,)), ((), ())),
                    preferred_element_type=jnp.float32,
                )
                * score_scale
            )
            key_pos = offset + jnp.arange(block_width, dtype=jnp.int32)
            visible = (key_pos[None, :] <= positions[:, None]) & (
                key_pos[None, :] >= begins[:, None]
            )
            visible = jnp.repeat(visible, group_size, axis=0)
            new_top = jnp.maximum(top_score, jnp.max(jnp.where(visible, scores, neg_big), axis=1))
            weights = jnp.where(visible, jnp.exp(scores - new_top[:, None]), 0.0)
            rescale = jnp.exp(top_score - new_top)
            denominator = denominator * rescale + jnp.sum(weights, axis=1)
            running = running * rescale[:, None] + jnp.dot(
                weights.astype(jnp.bfloat16), value_block, preferred_element_type=jnp.float32
            )
            return (new_top, denominator, running)

        result = lax.fori_loop(
            first_block,
            last_block,
            add_block,
            (top_scores[tile_num], denominators[tile_num], runnings[tile_num]),
        )
        new_tops.append(result[0])
        new_denoms.append(result[1])
        new_runs.append(result[2])
    return (jnp.stack(new_tops), jnp.stack(new_denoms), jnp.stack(new_runs))


def any_size(queries, keys, values, doc_lengths):
    by_head = lax.all_to_all(queries, "head", split_axis=1, concat_axis=0, tiled=True)
    tok_dev = by_head.shape[0]
    head_depth = keys.shape[1]
    group_size = by_head.shape[1] // head_depth
    tile_count = 8
    tok_rows = tok_dev // tile_count
    shard_index = lax.axis_index("ctx")
    doc_starts = jnp.cumsum(doc_lengths) - doc_lengths
    tile_query = by_head.reshape(tile_count, tok_rows * group_size, head_depth)
    tile_starts = shard_index * tok_dev + jnp.arange(tile_count, dtype=jnp.int32) * tok_rows
    query_rows = tok_rows * group_size
    initial = (
        jnp.full((tile_count, query_rows), neg_big, jnp.float32),
        jnp.zeros((tile_count, query_rows), jnp.float32),
        jnp.zeros((tile_count, query_rows, head_depth), jnp.float32),
    )
    whole_keys, whole_values = (
        lax.all_gather(keys, "ctx", axis=0, tiled=True),
        lax.all_gather(values, "ctx", axis=0, tiled=True),
    )
    carried = absorb(
        initial,
        tile_query,
        tile_starts,
        doc_starts,
        whole_keys,
        whole_values,
        jnp.int32(0),
        tok_rows,
    )
    results = (carried[2] / carried[1][..., None]).astype(jnp.bfloat16)
    merged = results.reshape(tok_dev, group_size * head_depth)
    return lax.all_to_all(merged, "head", split_axis=0, concat_axis=1, tiled=True)


def per_device(queries, keys, values, doc_lengths):
    out, norms = attend(queries, keys, values, doc_lengths)
    bound = jnp.max(norms[:4]) * jnp.max(norms[4:]) * exponent_scale**2
    return lax.cond(
        bound <= safe_exponent**2,
        lambda *_: out,
        any_size,
        queries,
        keys,
        values,
        doc_lengths,
    )


def solution(mesh):
    in_specs = (P(("ctx", "head"), None), P("ctx", "head"), P("ctx", "head"), P())
    out_specs = P(("ctx", "head"), None)
    return jax.shard_map(
        per_device, mesh=mesh, in_specs=in_specs, out_specs=out_specs, check_vma=False
    )
```

```python
import math

import jax
import jax.numpy as jnp
from jax import lax
from jax.experimental import pallas as pl
from jax.experimental.pallas import tpu as pltpu
from jax.sharding import PartitionSpec as P

neg_big = -1e30
block_keys = 512
MESH = pl.DeviceIdType.MESH

head_depth = 128
heads_per_group = 16
group_columns = heads_per_group * head_depth
own_tokens = 64
block = 256
row_keys = 4 * block
slot_columns = own_tokens * heads_per_group
exponent_scale = math.log2(math.e) / math.sqrt(head_depth)
safe_exponent = 100.0


def attend_kernel(
    q_ref,
    k_ref,
    v_ref,
    len_ref,
    out_ref,
    bound_ref,
    stage,
    keyval,
    q_in,
    q_cols,
    acc,
    denom,
    begins,
    o_part,
    stat_own,
    stat_in,
    stage_sem,
    chunk_sem,
    q_sem,
    o_sem,
    stat_sem,
    z_send,
    entry_send,
    x_send,
    y_send,
    q_send,
    sib_send,
    o_send,
    stat_send,
    own_sem,
):
    ctx = lax.axis_index("ctx")
    head = lax.axis_index("head")
    plane, y, x = ctx // 16, (ctx // 4) % 4, ctx % 4
    half, core = head // 2, head % 2
    yhi, xhi, ylo, xlo = y // 2, x // 2, y % 2, x % 2
    ybit, xbit = (ylo + yhi) % 2, (xlo + xhi) % 2
    group = ybit * 2 + xbit
    quad_row = plane * 4 + yhi * 2
    quad_pair = plane * 2 + yhi
    receiver = core == xbit
    same = (ybit == half).astype(jnp.int32)

    def ctx_of(p, yy, xx):
        return p * 16 + yy * 4 + xx

    sibling = (ctx, half * 2 + 1 - core)
    partners = [sibling, (ctx_of(plane, yhi * 2 + 1 - ylo, xhi * 2 + 1 - xlo), head)]
    for d in range(1, 4):
        partners.append((ctx_of(plane, y, (x + d) % 4), head))
        partners.append((ctx_of(plane, (y + d) % 4, x), head))
    for dz in range(1, 8):
        z = (half * 4 + plane + dz) % 8
        partners.append((ctx_of(z % 4, y, x), (z // 4) * 2 + core))
    barrier = pltpu.get_barrier_semaphore()
    for partner in partners:
        pl.semaphore_signal(barrier, inc=1, device_id=partner, device_id_type=MESH)

    mine = half * 4 + plane
    stage[mine, 0] = k_ref[...]
    v_t = v_ref[...].T
    stage[mine, 1] = jnp.concatenate([v_t[:, :128], v_t[:, 128:]], axis=0)
    own_slot = ylo * 2 + xlo

    lane = lax.broadcasted_iota(jnp.int32, (8, 128), 1) % own_tokens
    starts = []
    total = jnp.int32(0)
    for d in range(8):
        starts.append(total)
        total = total + len_ref[d]

    def slot_position(slot):
        c = ctx_of(plane, yhi * 2 + slot // 2, xhi * 2 + slot % 2)
        return c * block + head * own_tokens

    for slot in range(4):
        position = slot_position(slot) + lane
        begin = jnp.zeros((8, 128), jnp.int32)
        for start in starts:
            begin = jnp.maximum(begin, jnp.where(position >= start, start, 0))
        begins[slot] = begin

    acc[...] = jnp.zeros_like(acc)
    denom[...] = jnp.zeros_like(denom)
    own_keys = k_ref[...].astype(jnp.float32)
    key_norm = jnp.max(jnp.sum(own_keys * own_keys, axis=1))

    def columns_of(slot, read):
        best = jnp.zeros((1, 128), jnp.float32)
        for pair in range(8):
            two = read(pair)
            tile = jnp.concatenate([two[:, :128], two[:, 128:]], axis=0)
            turned = tile.astype(jnp.float32).T
            best = jnp.maximum(best, jnp.sum(turned * turned, axis=0, keepdims=True))
            at = pl.multiple_of(slot * slot_columns + pair * 128, 128)
            q_cols[:, pl.ds(at, 128)] = turned.astype(jnp.bfloat16)
        return best

    def read_own(pair):
        at = pl.multiple_of(group * group_columns + pair * 256, 128)
        return q_ref[:, pl.ds(at, 256)]

    query_norm = columns_of(own_slot, read_own)

    pl.semaphore_wait(barrier, len(partners))

    def remote(src, dst, send, recv, target):
        return pltpu.make_async_remote_copy(
            src_ref=src,
            dst_ref=dst,
            send_sem=send,
            recv_sem=recv,
            device_id=target,
            device_id_type=MESH,
        )

    def z_copy(n, index, to_half, to_plane):
        return remote(
            stage.at[index],
            stage.at[index],
            z_send.at[n],
            stage_sem.at[index],
            (ctx_of(to_plane, y, x), to_half * 2 + core),
        )

    def stage_index(flip, back):
        return ((half + flip) % 2) * 4 + plane - back

    z_hops = [
        (plane <= 3, 0, mine, 1 - half, jnp.minimum(plane + 1, 3)),
        (plane <= 2, 1, mine, half, plane + 1),
        (plane >= 1, 2, stage_index(1, 1), half, plane - 1),
        ((plane >= 1) & (plane <= 2), 3, stage_index(1, 1), half, plane + 1),
        ((plane >= 1) & (plane <= 2), 4, stage_index(0, 1), half, plane + 1),
    ]

    def z_start(n):
        pl.when(z_hops[n][0])(lambda: z_copy(*z_hops[n][1:]).start())

    def entry(flip, back, act):
        g = (half + flip) % 2
        p = plane - back
        index = stage_index(flip, back)
        to_y, to_x = yhi * 2 + (g + yhi) % 2, xhi * 2 + (core + xhi) % 2
        here = (to_y == y) & (to_x == x)
        pair = p * 2 + yhi
        target = keyval.at[pair, xhi, ylo, :, xlo]

        @pl.when((p >= 0) & jnp.logical_not(here))
        def _():
            copy = remote(
                stage.at[index],
                target,
                entry_send.at[flip * 3 + back],
                chunk_sem.at[pair * 2 + xhi],
                (ctx_of(plane, to_y, to_x), head),
            )
            copy.start() if act == "start" else copy.wait_send()

        if act == "start":

            @pl.when((p >= 0) & here)
            def _():
                pltpu.make_async_copy(
                    stage.at[index], target, chunk_sem.at[pair * 2 + xhi]
                ).start()

    def relay(flip, back, *hops):
        @pl.when(plane >= back)
        def _():
            z_copy(0, stage_index(flip, back), 1 - half, plane).wait_recv()

        for hop in hops:
            z_start(hop)
        entry(flip, back, "start")

    def mate(k):
        my, mx = (ylo + k // 2) % 2, (xlo + k % 2) % 2
        return my, mx

    def q_copy(k):
        my, mx = mate(k)
        to_group = ((my + yhi) % 2) * 2 + (mx + xhi) % 2
        columns = pl.ds(pl.multiple_of(to_group * group_columns, 128), group_columns)
        return remote(
            q_ref.at[:, columns],
            q_in.at[own_slot],
            q_send.at[k],
            q_sem.at[own_slot],
            (ctx_of(plane, yhi * 2 + my, xhi * 2 + mx), head),
        )

    def q_wait(k):
        my, mx = mate(k)
        slot = my * 2 + mx
        remote(q_in.at[slot], q_in.at[slot], q_send.at[0], q_sem.at[slot], sibling).wait_recv()

    z_start(0)
    z_start(1)
    entry(0, 0, "start")
    for k in (1, 2, 3):
        q_copy(k).start()

    def chunk_copy(pair, side, send, target):
        chunk = keyval.at[pair, side]
        return remote(chunk, chunk, send, chunk_sem.at[pair * 2 + side], target)

    def sib_copy(pair, side):
        return chunk_copy(pair, side, sib_send.at[pair * 2 + side], sibling)

    x_next = (ctx_of(plane, y, (1 - xhi) * 2 + (xbit + 1 - xhi) % 2), head)
    y_next = (ctx_of(plane, (1 - yhi) * 2 + (ybit + 1 - yhi) % 2, x), head)

    def sent_on(back):
        return ((back == 0) & (yhi == 0)) | (back == 1) | ((back == 2) & (yhi == 1))

    def got_from(back):
        return ((back == 0) & (yhi == 1)) | (back == 1) | ((back == 2) & (yhi == 0))

    def x_copy(back):
        return chunk_copy((plane - back) * 2 + yhi, xhi, x_send.at[back], x_next)

    def y_copy(back, side):
        pair = (plane - back) * 2 + yhi
        return chunk_copy(pair, (xhi + side) % 2, y_send.at[back * 2 + side], y_next)

    def take_own(back):
        pair = (plane - back) * 2 + yhi

        @pl.when(plane >= back)
        def _():
            sib_copy(pair, xhi).wait_recv()

            @pl.when(receiver)
            def _():
                x_copy(back).start()
                pl.when(sent_on(back))(lambda: y_copy(back, 0).start())
                sib_copy(pair, xhi).start()

    def take_x(back):
        pair = (plane - back) * 2 + yhi

        @pl.when(plane >= back)
        def _():
            sib_copy(pair, 1 - xhi).wait_recv()

            @pl.when(receiver)
            def _():
                pl.when(sent_on(back))(lambda: y_copy(back, 1).start())
                sib_copy(pair, 1 - xhi).start()

    def take_y(back, side):
        pair = (plane - back) * 2 + 1 - yhi

        @pl.when((plane >= back) & got_from(back))
        def _():
            sib_copy(pair, (xhi + side) % 2).wait_recv()
            pl.when(receiver)(lambda: sib_copy(pair, (xhi + side) % 2).start())

    near_half = same == 1
    relay(0, 1, 4)
    pl.when(near_half)(lambda: take_own(0))
    relay(0, 2)
    relay(1, 1, 2, 3)
    take_own(1)

    def norms(query_norm):
        rank = lax.broadcasted_iota(jnp.int32, (8, 128), 0)
        return jnp.where(rank < 4, jnp.broadcast_to(query_norm, (8, 128)), key_norm)

    stat_own[0] = norms(query_norm)

    def slot_of(k):
        my, mx = mate(k)
        return my * 2 + mx

    def take_queries(k):
        q_wait(k)
        slot = slot_of(k)
        best = columns_of(slot, lambda pair: q_in[slot, :, pl.ds(pair * 256, 256)])
        stat_own[0] = jnp.maximum(stat_own[0], norms(best))

    rounds = [[(0, sibling)], [], [], []]
    for d in range(1, 4):
        rounds[1].append((d, (ctx_of(plane, y, (x + d) % 4), head)))
        rounds[2].append((3 + d, (ctx_of(plane, (y + d) % 4, x), head)))
    for dz in range(1, 8):
        z = (half * 4 + plane + dz) % 8
        rounds[3].append((6 + dz, (ctx_of(z % 4, y, x), (z // 4) * 2 + core)))

    def stat_copy(r, n, target):
        return remote(stat_own.at[r], stat_in.at[n], stat_send.at[n], stat_sem.at[n], target)

    def stat_start(r):
        for n, target in rounds[r]:
            stat_copy(r, n, target).start()

    def stat_finish(r):
        best = stat_own[r]
        for n, target in rounds[r]:
            stat_copy(r, n, target).wait()
            best = jnp.maximum(best, stat_in[n])
        stat_own[r + 1] = best

    key_rank = lax.broadcasted_iota(jnp.int32, (block, 128), 0)

    def absorb_keys(slot, keys, values_t, masks):
        columns = pl.ds(pl.multiple_of(slot * slot_columns, 128), slot_columns)
        scores = jnp.dot(keys, q_cols[:, columns], preferred_element_type=jnp.float32)
        visible = jnp.concatenate(masks, axis=0)
        visible = jnp.concatenate([visible] * (slot_columns // 128), axis=1)
        weights = jnp.where(visible, jnp.exp2(scores * exponent_scale), 0.0)
        ones = jnp.ones((8, values_t.shape[1]), jnp.bfloat16)
        sums = jnp.dot(
            jnp.concatenate([values_t, ones], axis=0),
            weights.astype(jnp.bfloat16),
            preferred_element_type=jnp.float32,
        )
        acc[:, columns] += sums[:head_depth]
        denom[:, columns] += sums[head_depth:]

    def key_block(row, i):
        return keyval[row // 2, i // 2, row % 2, 0, i % 2]

    def value_block(row, i):
        tile = keyval[row // 2, i // 2, row % 2, 1, i % 2]
        return jnp.concatenate([tile[:128], tile[128:]], axis=1)

    def whole_blocks(slot, blocks):
        begin = begins[slot][:1]
        absorb_keys(
            slot,
            jnp.concatenate([key_block(row, i) for row, i in blocks], axis=0),
            jnp.concatenate([value_block(row, i) for row, i in blocks], axis=1),
            [key_rank + (row * row_keys + i * block) >= begin for row, i in blocks],
        )

    def full_row(row, slot):
        whole_blocks(slot, [(row, i) for i in range(4)])

    def full_chunk(pair, side, slot):
        blocks = [(pair * 2 + dy, side * 2 + dx) for dy in range(2) for dx in range(2)]
        whole_blocks(slot, blocks)

    def edge_rows(slot):
        slot_y, slot_x = yhi * 2 + slot // 2, xhi * 2 + slot % 2
        near = plane * 4 + slot_y
        far = near - 8
        there = (far >= 0).astype(jnp.int32)
        held = there * far + (1 - there) * near
        begin = begins[slot][:1]
        position = slot_position(slot) + lane[:1]
        keys, values_t, masks = [], [], []
        for i in range(4):
            is_near = (slot_x >= i).astype(jnp.int32)
            row = is_near * near + (1 - is_near) * held
            first = (is_near * near + (1 - is_near) * far) * row_keys + i * block
            keys.append(key_block(row, i))
            values_t.append(value_block(row, i))
            key = key_rank + first
            masks.append((key >= begin) & (key <= position))
        absorb_keys(slot, jnp.concatenate(keys, axis=0), jnp.concatenate(values_t, axis=1), masks)

        @pl.when(far >= 0)
        def _():
            first = far * row_keys + slot_x * block
            absorb_keys(
                slot,
                key_block(held, slot_x),
                value_block(held, slot_x),
                [key_rank + first >= begin],
            )

    def when_near(act, near):
        pl.when(same == near)(act)

    far_steps = {('relay', 0): 1, ('relay', 2): 2, ('own', 0): 4, ('own', 2): 5, ('x', 1): 4, ('y', 1, 0): 7, ('y', 1, 1): 11, ('x', 0): 13, ('x', 2): 14, ('y', 0, 0): 18, ('y', 2, 0): 18}
    near_steps = {('x', 0): 1, ('own', 2): 2, ('x', 1): 3, ('relay', 0): 4, ('relay', 2): 4, ('x', 2): 7, ('y', 1, 0): 7, ('y', 1, 1): 11, ('y', 0, 0): 18, ('y', 2, 0): 18}
    last_keys = [('y', 0, 1), ('y', 2, 1)]
    stat_steps = [6, 10, 15, 20]
    events = []
    for key, at in far_steps.items():
        events.append((at, 0, key))
    for key, at in near_steps.items():
        events.append((at, 1, key))

    def act_on(key):
        kind, back = key[0], key[1]
        if kind == "relay":
            relay(1, back)
        elif kind == "own":
            take_own(back)
        elif kind == "x":
            take_x(back)
        else:
            take_y(back, key[2])

    def before(step, at):
        here = [(near, key) for when, near, key in events if when == at]
        starts_here = [r for r in range(4) if stat_steps[r] == at]
        if here or starts_here or 1 <= at <= 3:

            @pl.when(step == at)
            def _():
                if 1 <= at <= 3:
                    take_queries(at)
                for near, key in here:
                    when_near(lambda key=key: act_on(key), near)
                for r in starts_here:
                    if r:
                        stat_finish(r - 1)
                    stat_start(r)

    first_y = yhi * -3 + (1 - yhi) * -1

    def chunk_step(chunk, k):
        side = (xhi + chunk) % 2
        order = chunk // 2
        back = jnp.where(order == 0, -2, jnp.where(order == 1, first_y, -4 - first_y))
        pair = quad_pair + back

        @pl.when(pair >= 0)
        def _():
            full_chunk(pair, side, slot_of(k))

    @pl.loop(0, 16)
    def _(step):
        for at in range(16):
            before(step, at)
        chunk_step(step // 4, step % 4)

    @pl.loop(16, 20)
    def _(step):
        for at in range(16, 20):
            before(step, at)
        slot = slot_of(step - 16)
        last = quad_row - 7 * (1 - slot // 2)

        @pl.when(last >= 0)
        def _():
            full_row(last, slot)

        edge_rows(slot)

    @pl.loop(20, 24)
    def _(step):
        for at in range(20, 24):
            before(step, at)
        chunk_step(jnp.int32(4), step - 20)

    for key in last_keys:
        act_on(key)
    def o_columns():
        return pl.ds(pl.multiple_of(group * group_columns, 128), group_columns)

    def o_copy(k):
        my, mx = mate(k)
        return remote(
            o_part.at[my * 2 + mx],
            out_ref.at[:, o_columns()],
            o_send.at[k],
            o_sem.at[k],
            (ctx_of(plane, yhi * 2 + my, xhi * 2 + mx), head),
        )

    def o_arrival(k):
        my, mx = mate(k)
        from_group = ((my + yhi) % 2) * 2 + (mx + xhi) % 2
        columns = pl.ds(pl.multiple_of(from_group * group_columns, 128), group_columns)
        return remote(
            o_part.at[own_slot], out_ref.at[:, columns], o_send.at[k], o_sem.at[k], sibling
        )

    for k in (3, 2, 1, 0):
        slot = slot_of(k)
        chunk_step(jnp.int32(5), jnp.int32(k))

        for pair in range(8):
            columns = pl.ds(pl.multiple_of(slot * slot_columns + pair * 128, 128), 128)
            share = acc[:, columns] / denom[:1, columns]
            back = share.T.astype(jnp.bfloat16)
            o_part[slot, :, pl.ds(pair * 256, 128)] = back[:own_tokens]
            o_part[slot, :, pl.ds(pair * 256 + 128, 128)] = back[own_tokens:]
        if k:
            o_copy(k).start()
    home = pltpu.make_async_copy(o_part.at[own_slot], out_ref.at[:, o_columns()], own_sem)
    home.start()
    stat_finish(3)
    bound_ref[0] = jnp.max(stat_own[4, :4]) * jnp.max(stat_own[4, 4:])

    for k in (1, 2, 3):
        q_copy(k).wait_send()
    for hop in z_hops:
        pl.when(hop[0])(lambda hop=hop: z_copy(*hop[1:]).wait_send())
    for flip in range(2):
        for back in range(3):
            entry(flip, back, "wait")
    for back in range(3):

        @pl.when((plane >= back) & receiver)
        def _():
            x_copy(back).wait_send()
            sib_copy((plane - back) * 2 + yhi, 0).wait_send()
            sib_copy((plane - back) * 2 + yhi, 1).wait_send()

            @pl.when(sent_on(back))
            def _():
                y_copy(back, 0).wait_send()
                y_copy(back, 1).wait_send()

            @pl.when(got_from(back))
            def _():
                sib_copy((plane - back) * 2 + 1 - yhi, 0).wait_send()
                sib_copy((plane - back) * 2 + 1 - yhi, 1).wait_send()

    for k in (3, 2, 1):
        o_copy(k).wait_send()
        o_arrival(k).wait_recv()
    home.wait()


def attend(queries, keys, values, doc_lengths):
    vmem = pl.BlockSpec(memory_space=pltpu.VMEM)
    smem = pl.BlockSpec(memory_space=pltpu.SMEM)
    elements = 9 * row_keys * 4 * slot_columns
    dma = pltpu.SemaphoreType.DMA
    return pl.pallas_call(
        attend_kernel,
        name="attend",
        out_shape=(
            jax.ShapeDtypeStruct(queries.shape, jnp.bfloat16),
            jax.ShapeDtypeStruct((1,), jnp.float32),
        ),
        in_specs=[vmem, vmem, vmem, smem],
        out_specs=(vmem, smem),
        scratch_shapes=[
            pltpu.VMEM((8, 2, block, head_depth), jnp.bfloat16),
            pltpu.VMEM((8, 2, 2, 2, 2, block, head_depth), jnp.bfloat16),
            pltpu.VMEM((4, own_tokens, group_columns), jnp.bfloat16),
            pltpu.VMEM((head_depth, 4 * slot_columns), jnp.bfloat16),
            pltpu.VMEM((head_depth, 4 * slot_columns), jnp.float32),
            pltpu.VMEM((8, 4 * slot_columns), jnp.float32),
            pltpu.VMEM((4, 8, 128), jnp.int32),
            pltpu.VMEM((4, own_tokens, group_columns), jnp.bfloat16),
            pltpu.VMEM((5, 8, 128), jnp.float32),
            pltpu.VMEM((14, 8, 128), jnp.float32),
            dma((8,)),
            dma((16,)),
            dma((4,)),
            dma((4,)),
            dma((14,)),
            dma((5,)),
            dma((6,)),
            dma((3,)),
            dma((6,)),
            dma((4,)),
            dma((16,)),
            dma((4,)),
            dma((14,)),
            dma,
        ],
        compiler_params=pltpu.CompilerParams(
            collective_id=0, has_side_effects=True, vmem_limit_bytes=56 << 20
        ),
        cost_estimate=pl.CostEstimate(
            flops=4 * elements * head_depth, bytes_accessed=4 << 20, transcendentals=elements
        ),
    )(queries, keys, values, doc_lengths)


def token_begins(doc_starts, positions):
    hit = doc_starts[None, :] <= positions[:, None]
    return jnp.max(jnp.where(hit, doc_starts[None, :], 0), axis=1)


def absorb(
    carried, held_tiles, tile_starts, doc_starts, key_piece, value_piece, piece_start, tok_rows
):
    top_scores, denominators, runnings = carried
    piece_rows = key_piece.shape[0]
    block_width = math.gcd(piece_rows, block_keys)
    tile_count, query_rows, head_depth = held_tiles.shape
    group_size = query_rows // tok_rows
    score_scale = 1.0 / math.sqrt(head_depth)
    new_tops, new_denoms, new_runs = ([], [], [])
    for tile_num in range(tile_count):
        tile_start = tile_starts[tile_num]
        positions = tile_start + jnp.arange(tok_rows, dtype=jnp.int32)
        begins = token_begins(doc_starts, positions)
        low_pos = jnp.maximum(begins[0], piece_start)
        high_pos = jnp.minimum(tile_start + tok_rows, piece_start + piece_rows)
        first_block = low_pos // block_width
        last_block = jnp.maximum(first_block, (high_pos + block_width - 1) // block_width)
        tile_query = held_tiles[tile_num]

        def add_block(block_index, loop_state):
            top_score, denominator, running = loop_state
            offset = block_index * block_width
            key_block = lax.dynamic_slice_in_dim(key_piece, offset, block_width, 0)
            value_block = lax.dynamic_slice_in_dim(value_piece, offset, block_width, 0)
            scores = (
                lax.dot_general(
                    tile_query,
                    key_block,
                    (((1,), (1,)), ((), ())),
                    preferred_element_type=jnp.float32,
                )
                * score_scale
            )
            key_pos = offset + jnp.arange(block_width, dtype=jnp.int32)
            visible = (key_pos[None, :] <= positions[:, None]) & (
                key_pos[None, :] >= begins[:, None]
            )
            visible = jnp.repeat(visible, group_size, axis=0)
            new_top = jnp.maximum(top_score, jnp.max(jnp.where(visible, scores, neg_big), axis=1))
            weights = jnp.where(visible, jnp.exp(scores - new_top[:, None]), 0.0)
            rescale = jnp.exp(top_score - new_top)
            denominator = denominator * rescale + jnp.sum(weights, axis=1)
            running = running * rescale[:, None] + jnp.dot(
                weights.astype(jnp.bfloat16), value_block, preferred_element_type=jnp.float32
            )
            return (new_top, denominator, running)

        result = lax.fori_loop(
            first_block,
            last_block,
            add_block,
            (top_scores[tile_num], denominators[tile_num], runnings[tile_num]),
        )
        new_tops.append(result[0])
        new_denoms.append(result[1])
        new_runs.append(result[2])
    return (jnp.stack(new_tops), jnp.stack(new_denoms), jnp.stack(new_runs))


def from_all(piece):
    copies = jnp.tile(piece, (lax.axis_size("ctx"), 1))
    return lax.all_to_all(copies, "ctx", split_axis=0, concat_axis=0, tiled=True)


def any_size(queries, keys, values, doc_lengths):
    by_head = lax.all_to_all(queries, "head", split_axis=1, concat_axis=0, tiled=True)
    tok_dev = by_head.shape[0]
    head_depth = keys.shape[1]
    group_size = by_head.shape[1] // head_depth
    tile_count = 8
    tok_rows = tok_dev // tile_count
    shard_index = lax.axis_index("ctx")
    doc_starts = jnp.cumsum(doc_lengths) - doc_lengths
    tile_query = by_head.reshape(tile_count, tok_rows * group_size, head_depth)
    tile_starts = shard_index * tok_dev + jnp.arange(tile_count, dtype=jnp.int32) * tok_rows
    query_rows = tok_rows * group_size
    initial = (
        jnp.full((tile_count, query_rows), neg_big, jnp.float32),
        jnp.zeros((tile_count, query_rows), jnp.float32),
        jnp.zeros((tile_count, query_rows, head_depth), jnp.float32),
    )
    whole_keys, whole_values = (
        from_all(keys),
        from_all(values),
    )
    carried = absorb(
        initial,
        tile_query,
        tile_starts,
        doc_starts,
        whole_keys,
        whole_values,
        jnp.int32(0),
        tok_rows,
    )
    results = (carried[2] / carried[1][..., None]).astype(jnp.bfloat16)
    merged = results.reshape(tok_dev, group_size * head_depth)
    return lax.all_to_all(merged, "head", split_axis=0, concat_axis=1, tiled=True)


def per_device(queries, keys, values, doc_lengths):
    out, bound = attend(queries, keys, values, doc_lengths)
    return lax.cond(
        bound[0] <= (safe_exponent / exponent_scale) ** 2,
        lambda *_: out,
        any_size,
        queries,
        keys,
        values,
        doc_lengths,
    )


def solution(mesh):
    in_specs = (P(("ctx", "head"), None), P("ctx", "head"), P("ctx", "head"), P())
    out_specs = P(("ctx", "head"), None)
    return jax.shard_map(
        per_device, mesh=mesh, in_specs=in_specs, out_specs=out_specs, check_vma=False
    )
```

```python
import math

import jax
import jax.numpy as jnp
from jax import lax
from jax.experimental import pallas as pl
from jax.experimental.pallas import tpu as pltpu
from jax.sharding import PartitionSpec as P

neg_big = -1e30
block_keys = 512
MESH = pl.DeviceIdType.MESH

head_depth = 128
heads_per_group = 16
group_columns = heads_per_group * head_depth
own_tokens = 64
block = 256
row_keys = 4 * block
slot_columns = own_tokens * heads_per_group
exponent_scale = math.log2(math.e) / math.sqrt(head_depth)
safe_exponent = 100.0


def attend_kernel(
    q_ref,
    k_ref,
    v_ref,
    len_ref,
    out_ref,
    bound_ref,
    stage,
    keyval,
    q_in,
    q_cols,
    acc,
    denom,
    begins,
    o_part,
    stat_own,
    stat_in,
    stage_sem,
    chunk_sem,
    q_sem,
    o_sem,
    stat_sem,
    z_send,
    entry_send,
    x_send,
    y_send,
    q_send,
    sib_send,
    o_send,
    stat_send,
    own_sem,
):
    ctx = lax.axis_index("ctx")
    head = lax.axis_index("head")
    plane, y, x = ctx // 16, (ctx // 4) % 4, ctx % 4
    half, core = head // 2, head % 2
    yhi, xhi, ylo, xlo = y // 2, x // 2, y % 2, x % 2
    ybit, xbit = (ylo + yhi) % 2, (xlo + xhi) % 2
    group = ybit * 2 + xbit
    quad_row = plane * 4 + yhi * 2
    quad_pair = plane * 2 + yhi
    receiver = core == xbit
    same = (ybit == half).astype(jnp.int32)

    def ctx_of(p, yy, xx):
        return p * 16 + yy * 4 + xx

    sibling = (ctx, half * 2 + 1 - core)
    partners = [sibling, (ctx_of(plane, yhi * 2 + 1 - ylo, xhi * 2 + 1 - xlo), head)]
    for d in range(1, 4):
        partners.append((ctx_of(plane, y, (x + d) % 4), head))
        partners.append((ctx_of(plane, (y + d) % 4, x), head))
    for dz in range(1, 8):
        z = (half * 4 + plane + dz) % 8
        partners.append((ctx_of(z % 4, y, x), (z // 4) * 2 + core))
    barrier = pltpu.get_barrier_semaphore()
    for partner in partners:
        pl.semaphore_signal(barrier, inc=1, device_id=partner, device_id_type=MESH)

    mine = half * 4 + plane
    stage[mine, 0] = k_ref[...]
    v_t = v_ref[...].T
    stage[mine, 1] = jnp.concatenate([v_t[:, :128], v_t[:, 128:]], axis=0)
    own_slot = ylo * 2 + xlo

    lane = lax.broadcasted_iota(jnp.int32, (8, 128), 1) % own_tokens
    starts = []
    total = jnp.int32(0)
    for d in range(8):
        starts.append(total)
        total = total + len_ref[d]

    def slot_position(slot):
        c = ctx_of(plane, yhi * 2 + slot // 2, xhi * 2 + slot % 2)
        return c * block + head * own_tokens

    for slot in range(4):
        position = slot_position(slot) + lane
        begin = jnp.zeros((8, 128), jnp.int32)
        for start in starts:
            begin = jnp.maximum(begin, jnp.where(position >= start, start, 0))
        begins[slot] = begin

    acc[...] = jnp.zeros_like(acc)
    denom[...] = jnp.zeros_like(denom)
    own_keys = k_ref[...].astype(jnp.float32)
    key_norm = jnp.max(jnp.sum(own_keys * own_keys, axis=1))

    def columns_of(slot, read):
        best = jnp.zeros((1, 128), jnp.float32)
        for pair in range(8):
            two = read(pair)
            tile = jnp.concatenate([two[:, :128], two[:, 128:]], axis=0)
            turned = tile.astype(jnp.float32).T
            best = jnp.maximum(best, jnp.sum(turned * turned, axis=0, keepdims=True))
            at = pl.multiple_of(slot * slot_columns + pair * 128, 128)
            q_cols[:, pl.ds(at, 128)] = turned.astype(jnp.bfloat16)
        return best

    def read_own(pair):
        at = pl.multiple_of(group * group_columns + pair * 256, 128)
        return q_ref[:, pl.ds(at, 256)]

    query_norm = columns_of(own_slot, read_own)

    pl.semaphore_wait(barrier, len(partners))

    def remote(src, dst, send, recv, target):
        return pltpu.make_async_remote_copy(
            src_ref=src,
            dst_ref=dst,
            send_sem=send,
            recv_sem=recv,
            device_id=target,
            device_id_type=MESH,
        )

    def z_copy(n, index, to_half, to_plane):
        return remote(
            stage.at[index],
            stage.at[index],
            z_send.at[n],
            stage_sem.at[index],
            (ctx_of(to_plane, y, x), to_half * 2 + core),
        )

    def stage_index(flip, back):
        return ((half + flip) % 2) * 4 + plane - back

    z_hops = [
        (plane <= 3, 0, mine, 1 - half, jnp.minimum(plane + 1, 3)),
        (plane <= 2, 1, mine, half, plane + 1),
        (plane >= 1, 2, stage_index(1, 1), half, plane - 1),
        ((plane >= 1) & (plane <= 2), 3, stage_index(1, 1), half, plane + 1),
        ((plane >= 1) & (plane <= 2), 4, stage_index(0, 1), half, plane + 1),
    ]

    def z_start(n):
        pl.when(z_hops[n][0])(lambda: z_copy(*z_hops[n][1:]).start())

    def entry(flip, back, act):
        g = (half + flip) % 2
        p = plane - back
        index = stage_index(flip, back)
        to_y, to_x = yhi * 2 + (g + yhi) % 2, xhi * 2 + (core + xhi) % 2
        here = (to_y == y) & (to_x == x)
        pair = p * 2 + yhi
        target = keyval.at[pair, xhi, ylo, :, xlo]

        @pl.when((p >= 0) & jnp.logical_not(here))
        def _():
            copy = remote(
                stage.at[index],
                target,
                entry_send.at[flip * 3 + back],
                chunk_sem.at[pair * 2 + xhi],
                (ctx_of(plane, to_y, to_x), head),
            )
            copy.start() if act == "start" else copy.wait_send()

        if act == "start":

            @pl.when((p >= 0) & here)
            def _():
                pltpu.make_async_copy(
                    stage.at[index], target, chunk_sem.at[pair * 2 + xhi]
                ).start()

    def relay(flip, back, *hops):
        @pl.when(plane >= back)
        def _():
            z_copy(0, stage_index(flip, back), 1 - half, plane).wait_recv()

        for hop in hops:
            z_start(hop)
        entry(flip, back, "start")

    def mate(k):
        my, mx = (ylo + k // 2) % 2, (xlo + k % 2) % 2
        return my, mx

    def q_copy(k):
        my, mx = mate(k)
        to_group = ((my + yhi) % 2) * 2 + (mx + xhi) % 2
        columns = pl.ds(pl.multiple_of(to_group * group_columns, 128), group_columns)
        return remote(
            q_ref.at[:, columns],
            q_in.at[own_slot],
            q_send.at[k],
            q_sem.at[own_slot],
            (ctx_of(plane, yhi * 2 + my, xhi * 2 + mx), head),
        )

    def q_wait(k):
        my, mx = mate(k)
        slot = my * 2 + mx
        remote(q_in.at[slot], q_in.at[slot], q_send.at[0], q_sem.at[slot], sibling).wait_recv()

    middle = (plane == 1) | (plane == 2)
    pl.when(middle)(lambda: z_start(0))
    z_start(1)
    entry(0, 0, "start")
    for k in (1, 2, 3):
        q_copy(k).start()

    def chunk_copy(pair, side, send, target):
        chunk = keyval.at[pair, side]
        return remote(chunk, chunk, send, chunk_sem.at[pair * 2 + side], target)

    def sib_copy(pair, side):
        return chunk_copy(pair, side, sib_send.at[pair * 2 + side], sibling)

    x_next = (ctx_of(plane, y, (1 - xhi) * 2 + (xbit + 1 - xhi) % 2), head)
    y_next = (ctx_of(plane, (1 - yhi) * 2 + (ybit + 1 - yhi) % 2, x), head)

    def sent_on(back):
        return ((back == 0) & (yhi == 0)) | (back == 1) | ((back == 2) & (yhi == 1))

    def got_from(back):
        return ((back == 0) & (yhi == 1)) | (back == 1) | ((back == 2) & (yhi == 0))

    def x_copy(back):
        return chunk_copy((plane - back) * 2 + yhi, xhi, x_send.at[back], x_next)

    def y_copy(back, side):
        pair = (plane - back) * 2 + yhi
        return chunk_copy(pair, (xhi + side) % 2, y_send.at[back * 2 + side], y_next)

    def take_own(back):
        pair = (plane - back) * 2 + yhi

        @pl.when(plane >= back)
        def _():
            sib_copy(pair, xhi).wait_recv()

            @pl.when(receiver)
            def _():
                x_copy(back).start()
                pl.when(sent_on(back))(lambda: y_copy(back, 0).start())
                sib_copy(pair, xhi).start()

    def take_x(back):
        pair = (plane - back) * 2 + yhi

        @pl.when(plane >= back)
        def _():
            sib_copy(pair, 1 - xhi).wait_recv()

            @pl.when(receiver)
            def _():
                pl.when(sent_on(back))(lambda: y_copy(back, 1).start())
                sib_copy(pair, 1 - xhi).start()

    def take_y(back, side):
        pair = (plane - back) * 2 + 1 - yhi

        @pl.when((plane >= back) & got_from(back))
        def _():
            sib_copy(pair, (xhi + side) % 2).wait_recv()
            pl.when(receiver)(lambda: sib_copy(pair, (xhi + side) % 2).start())

    near_half = same == 1

    @pl.when(plane == 0)
    def _():
        z_copy(*z_hops[1][1:]).wait_send()
        z_start(0)

    relay(0, 1, 4)
    pl.when(near_half & (yhi == 0))(lambda: take_own(0))
    relay(1, 1, 2, 3)
    pl.when(plane == 3)(lambda: z_start(0))
    relay(0, 2)
    take_own(1)

    def norms(query_norm):
        rank = lax.broadcasted_iota(jnp.int32, (8, 128), 0)
        return jnp.where(rank < 4, jnp.broadcast_to(query_norm, (8, 128)), key_norm)

    stat_own[0] = norms(query_norm)

    def slot_of(k):
        my, mx = mate(k)
        return my * 2 + mx

    def take_queries(k):
        q_wait(k)
        slot = slot_of(k)
        best = columns_of(slot, lambda pair: q_in[slot, :, pl.ds(pair * 256, 256)])
        stat_own[0] = jnp.maximum(stat_own[0], norms(best))

    rounds = [[(0, sibling)], [], [], []]
    for d in range(1, 4):
        rounds[1].append((d, (ctx_of(plane, y, (x + d) % 4), head)))
        rounds[2].append((3 + d, (ctx_of(plane, (y + d) % 4, x), head)))
    for dz in range(1, 8):
        z = (half * 4 + plane + dz) % 8
        rounds[3].append((6 + dz, (ctx_of(z % 4, y, x), (z // 4) * 2 + core)))

    def stat_copy(r, n, target):
        return remote(stat_own.at[r], stat_in.at[n], stat_send.at[n], stat_sem.at[n], target)

    def stat_start(r):
        for n, target in rounds[r]:
            stat_copy(r, n, target).start()

    def stat_finish(r):
        best = stat_own[r]
        for n, target in rounds[r]:
            stat_copy(r, n, target).wait()
            best = jnp.maximum(best, stat_in[n])
        stat_own[r + 1] = best

    key_rank = lax.broadcasted_iota(jnp.int32, (block, 128), 0)

    def absorb_keys(slot, keys, values_t, masks):
        columns = pl.ds(pl.multiple_of(slot * slot_columns, 128), slot_columns)
        scores = jnp.dot(keys, q_cols[:, columns], preferred_element_type=jnp.float32)
        visible = jnp.concatenate(masks, axis=0)
        visible = jnp.concatenate([visible] * (slot_columns // 128), axis=1)
        weights = jnp.where(visible, jnp.exp2(scores * exponent_scale), 0.0)
        ones = jnp.ones((8, values_t.shape[1]), jnp.bfloat16)
        sums = jnp.dot(
            jnp.concatenate([values_t, ones], axis=0),
            weights.astype(jnp.bfloat16),
            preferred_element_type=jnp.float32,
        )
        acc[:, columns] += sums[:head_depth]
        denom[:, columns] += sums[head_depth:]

    def key_block(row, i):
        return keyval[row // 2, i // 2, row % 2, 0, i % 2]

    def value_block(row, i):
        tile = keyval[row // 2, i // 2, row % 2, 1, i % 2]
        return jnp.concatenate([tile[:128], tile[128:]], axis=1)

    def whole_blocks(slot, blocks):
        begin = begins[slot][:1]
        absorb_keys(
            slot,
            jnp.concatenate([key_block(row, i) for row, i in blocks], axis=0),
            jnp.concatenate([value_block(row, i) for row, i in blocks], axis=1),
            [key_rank + (row * row_keys + i * block) >= begin for row, i in blocks],
        )

    def full_row(row, slot):
        whole_blocks(slot, [(row, i) for i in range(4)])

    def full_chunk(pair, side, slot):
        blocks = [(pair * 2 + dy, side * 2 + dx) for dy in range(2) for dx in range(2)]
        whole_blocks(slot, blocks)

    def edge_rows(slot):
        slot_y, slot_x = yhi * 2 + slot // 2, xhi * 2 + slot % 2
        near = plane * 4 + slot_y
        far = near - 8
        there = (far >= 0).astype(jnp.int32)
        held = there * far + (1 - there) * near
        begin = begins[slot][:1]
        position = slot_position(slot) + lane[:1]
        keys, values_t, masks = [], [], []
        for i in range(4):
            is_near = (slot_x >= i).astype(jnp.int32)
            row = is_near * near + (1 - is_near) * held
            first = (is_near * near + (1 - is_near) * far) * row_keys + i * block
            keys.append(key_block(row, i))
            values_t.append(value_block(row, i))
            key = key_rank + first
            masks.append((key >= begin) & (key <= position))
        absorb_keys(slot, jnp.concatenate(keys, axis=0), jnp.concatenate(values_t, axis=1), masks)

        @pl.when(far >= 0)
        def _():
            first = far * row_keys + slot_x * block
            absorb_keys(
                slot,
                key_block(held, slot_x),
                value_block(held, slot_x),
                [key_rank + first >= begin],
            )

    def when_near(act, near):
        pl.when(same == near)(act)

    far_steps = {('relay', 0): 1, ('relay', 2): 2, ('x', 1): 4, ('own', 'first'): 6, ('y', 1, 0): 7, ('own', 'second'): 9, ('x', 'first'): 10, ('y', 1, 1): 11, ('x', 'second'): 15, ('y', 'second', 0): 16}
    near_steps = {('own', 'first'): 2, ('relay', 0): 2, ('relay', 2): 3, ('x', 1): 3, ('own', 'second'): 5, ('x', 'first'): 7, ('y', 1, 0): 7, ('y', 1, 1): 10, ('x', 'second'): 11, ('y', 'second', 0): 16}
    stat_steps = [5, 8, 12, 15]
    events = []
    for key, at in far_steps.items():
        events.append((at, 0, key))
    for key, at in near_steps.items():
        events.append((at, 1, key))

    def act_on(key):
        kind, back = key[0], key[1]
        if back == "first":
            back = 2 * yhi
        elif back == "second":
            back = 2 - 2 * yhi
        if kind == "relay":
            relay(1, back)
        elif kind == "own":
            early = (same == 1) & (yhi == 0) & (back == 0)
            pl.when(jnp.logical_not(early))(lambda: take_own(back))
        elif kind == "x":
            take_x(back)
        else:
            take_y(back, key[2])

    def before(step, at):
        here = [(near, key) for when, near, key in events if when == at]
        starts_here = [r for r in range(4) if stat_steps[r] == at]
        if here or starts_here or 1 <= at <= 3:

            @pl.when(step == at)
            def _():
                if 1 <= at <= 3:
                    take_queries(at)
                for near, key in here:
                    when_near(lambda key=key: act_on(key), near)
                for r in starts_here:
                    if r:
                        stat_finish(r - 1)
                    stat_start(r)

    first_y = yhi * -3 + (1 - yhi) * -1

    def chunk_step(chunk, k):
        side = (xhi + chunk) % 2
        order = chunk // 2
        back = jnp.where(order == 0, -2, jnp.where(order == 1, first_y, -4 - first_y))
        pair = quad_pair + back

        @pl.when(pair >= 0)
        def _():
            full_chunk(pair, side, slot_of(k))

    @pl.loop(0, 16)
    def _(step):
        for at in range(16):
            before(step, at)
        chunk_step(step // 4, step % 4)

    def edge_step(slot):
        last = quad_row - 7 * (1 - slot // 2)

        @pl.when(last >= 0)
        def _():
            full_row(last, slot)

        edge_rows(slot)

    @pl.loop(16, 18)
    def _(step):
        for at in range(16, 18):
            before(step, at)
        edge_step(slot_of(19 - step))

    act_on(("y", "second", 1))

    def o_columns():
        return pl.ds(pl.multiple_of(group * group_columns, 128), group_columns)

    def o_copy(k):
        my, mx = mate(k)
        return remote(
            o_part.at[my * 2 + mx],
            out_ref.at[:, o_columns()],
            o_send.at[k],
            o_sem.at[k],
            (ctx_of(plane, yhi * 2 + my, xhi * 2 + mx), head),
        )

    def o_arrival(k):
        my, mx = mate(k)
        from_group = ((my + yhi) % 2) * 2 + (mx + xhi) % 2
        columns = pl.ds(pl.multiple_of(from_group * group_columns, 128), group_columns)
        return remote(
            o_part.at[own_slot], out_ref.at[:, columns], o_send.at[k], o_sem.at[k], sibling
        )

    @pl.loop(0, 4)
    def _(turn):
        k = 3 - turn
        slot = slot_of(k)
        pl.when(turn >= 2)(lambda: edge_step(slot))

        @pl.loop(4, 6)
        def _(chunk):
            chunk_step(chunk, k)

        for pair in range(8):
            columns = pl.ds(pl.multiple_of(slot * slot_columns + pair * 128, 128), 128)
            share = acc[:, columns] / denom[:1, columns]
            back = share.T.astype(jnp.bfloat16)
            o_part[slot, :, pl.ds(pair * 256, 128)] = back[:own_tokens]
            o_part[slot, :, pl.ds(pair * 256 + 128, 128)] = back[own_tokens:]
        pl.when(k > 0)(lambda: o_copy(k).start())

    home = pltpu.make_async_copy(o_part.at[own_slot], out_ref.at[:, o_columns()], own_sem)
    home.start()
    stat_finish(3)
    bound_ref[0] = jnp.max(stat_own[4, :4]) * jnp.max(stat_own[4, 4:])

    for k in (1, 2, 3):
        q_copy(k).wait_send()
    for n, hop in enumerate(z_hops):
        left = hop[0] & (plane > 0) if n == 1 else hop[0]
        pl.when(left)(lambda hop=hop: z_copy(*hop[1:]).wait_send())
    for flip in range(2):
        for back in range(3):
            entry(flip, back, "wait")
    for back in range(3):

        @pl.when((plane >= back) & receiver)
        def _():
            x_copy(back).wait_send()
            sib_copy((plane - back) * 2 + yhi, 0).wait_send()
            sib_copy((plane - back) * 2 + yhi, 1).wait_send()

            @pl.when(sent_on(back))
            def _():
                y_copy(back, 0).wait_send()
                y_copy(back, 1).wait_send()

            @pl.when(got_from(back))
            def _():
                sib_copy((plane - back) * 2 + 1 - yhi, 0).wait_send()
                sib_copy((plane - back) * 2 + 1 - yhi, 1).wait_send()

    for k in (3, 2, 1):
        o_copy(k).wait_send()
        o_arrival(k).wait_recv()
    home.wait()


def attend(queries, keys, values, doc_lengths):
    vmem = pl.BlockSpec(memory_space=pltpu.VMEM)
    smem = pl.BlockSpec(memory_space=pltpu.SMEM)
    elements = 9 * row_keys * 4 * slot_columns
    dma = pltpu.SemaphoreType.DMA
    return pl.pallas_call(
        attend_kernel,
        name="attend",
        out_shape=(
            jax.ShapeDtypeStruct(queries.shape, jnp.bfloat16),
            jax.ShapeDtypeStruct((1,), jnp.float32),
        ),
        in_specs=[vmem, vmem, vmem, smem],
        out_specs=(vmem, smem),
        scratch_shapes=[
            pltpu.VMEM((8, 2, block, head_depth), jnp.bfloat16),
            pltpu.VMEM((8, 2, 2, 2, 2, block, head_depth), jnp.bfloat16),
            pltpu.VMEM((4, own_tokens, group_columns), jnp.bfloat16),
            pltpu.VMEM((head_depth, 4 * slot_columns), jnp.bfloat16),
            pltpu.VMEM((head_depth, 4 * slot_columns), jnp.float32),
            pltpu.VMEM((8, 4 * slot_columns), jnp.float32),
            pltpu.VMEM((4, 8, 128), jnp.int32),
            pltpu.VMEM((4, own_tokens, group_columns), jnp.bfloat16),
            pltpu.VMEM((5, 8, 128), jnp.float32),
            pltpu.VMEM((14, 8, 128), jnp.float32),
            dma((8,)),
            dma((16,)),
            dma((4,)),
            dma((4,)),
            dma((14,)),
            dma((5,)),
            dma((6,)),
            dma((3,)),
            dma((6,)),
            dma((4,)),
            dma((16,)),
            dma((4,)),
            dma((14,)),
            dma,
        ],
        compiler_params=pltpu.CompilerParams(
            collective_id=0, has_side_effects=True, vmem_limit_bytes=56 << 20
        ),
        cost_estimate=pl.CostEstimate(
            flops=4 * elements * head_depth, bytes_accessed=4 << 20, transcendentals=elements
        ),
    )(queries, keys, values, doc_lengths)


def token_begins(doc_starts, positions):
    hit = doc_starts[None, :] <= positions[:, None]
    return jnp.max(jnp.where(hit, doc_starts[None, :], 0), axis=1)


def absorb(
    carried, held_tiles, tile_starts, doc_starts, key_piece, value_piece, piece_start, tok_rows
):
    top_scores, denominators, runnings = carried
    piece_rows = key_piece.shape[0]
    block_width = math.gcd(piece_rows, block_keys)
    tile_count, query_rows, head_depth = held_tiles.shape
    group_size = query_rows // tok_rows
    score_scale = 1.0 / math.sqrt(head_depth)
    new_tops, new_denoms, new_runs = ([], [], [])
    for tile_num in range(tile_count):
        tile_start = tile_starts[tile_num]
        positions = tile_start + jnp.arange(tok_rows, dtype=jnp.int32)
        begins = token_begins(doc_starts, positions)
        low_pos = jnp.maximum(begins[0], piece_start)
        high_pos = jnp.minimum(tile_start + tok_rows, piece_start + piece_rows)
        first_block = low_pos // block_width
        last_block = jnp.maximum(first_block, (high_pos + block_width - 1) // block_width)
        tile_query = held_tiles[tile_num]

        def add_block(block_index, loop_state):
            top_score, denominator, running = loop_state
            offset = block_index * block_width
            key_block = lax.dynamic_slice_in_dim(key_piece, offset, block_width, 0)
            value_block = lax.dynamic_slice_in_dim(value_piece, offset, block_width, 0)
            scores = (
                lax.dot_general(
                    tile_query,
                    key_block,
                    (((1,), (1,)), ((), ())),
                    preferred_element_type=jnp.float32,
                )
                * score_scale
            )
            key_pos = offset + jnp.arange(block_width, dtype=jnp.int32)
            visible = (key_pos[None, :] <= positions[:, None]) & (
                key_pos[None, :] >= begins[:, None]
            )
            visible = jnp.repeat(visible, group_size, axis=0)
            new_top = jnp.maximum(top_score, jnp.max(jnp.where(visible, scores, neg_big), axis=1))
            weights = jnp.where(visible, jnp.exp(scores - new_top[:, None]), 0.0)
            rescale = jnp.exp(top_score - new_top)
            denominator = denominator * rescale + jnp.sum(weights, axis=1)
            running = running * rescale[:, None] + jnp.dot(
                weights.astype(jnp.bfloat16), value_block, preferred_element_type=jnp.float32
            )
            return (new_top, denominator, running)

        result = lax.fori_loop(
            first_block,
            last_block,
            add_block,
            (top_scores[tile_num], denominators[tile_num], runnings[tile_num]),
        )
        new_tops.append(result[0])
        new_denoms.append(result[1])
        new_runs.append(result[2])
    return (jnp.stack(new_tops), jnp.stack(new_denoms), jnp.stack(new_runs))


def from_all(piece):
    copies = jnp.tile(piece, (lax.axis_size("ctx"), 1))
    return lax.all_to_all(copies, "ctx", split_axis=0, concat_axis=0, tiled=True)


def any_size(queries, keys, values, doc_lengths):
    by_head = lax.all_to_all(queries, "head", split_axis=1, concat_axis=0, tiled=True)
    tok_dev = by_head.shape[0]
    head_depth = keys.shape[1]
    group_size = by_head.shape[1] // head_depth
    tile_count = 8
    tok_rows = tok_dev // tile_count
    shard_index = lax.axis_index("ctx")
    doc_starts = jnp.cumsum(doc_lengths) - doc_lengths
    tile_query = by_head.reshape(tile_count, tok_rows * group_size, head_depth)
    tile_starts = shard_index * tok_dev + jnp.arange(tile_count, dtype=jnp.int32) * tok_rows
    query_rows = tok_rows * group_size
    initial = (
        jnp.full((tile_count, query_rows), neg_big, jnp.float32),
        jnp.zeros((tile_count, query_rows), jnp.float32),
        jnp.zeros((tile_count, query_rows, head_depth), jnp.float32),
    )
    whole_keys, whole_values = (
        from_all(keys),
        from_all(values),
    )
    carried = absorb(
        initial,
        tile_query,
        tile_starts,
        doc_starts,
        whole_keys,
        whole_values,
        jnp.int32(0),
        tok_rows,
    )
    results = (carried[2] / carried[1][..., None]).astype(jnp.bfloat16)
    merged = results.reshape(tok_dev, group_size * head_depth)
    return lax.all_to_all(merged, "head", split_axis=0, concat_axis=1, tiled=True)


def per_device(queries, keys, values, doc_lengths):
    out, bound = attend(queries, keys, values, doc_lengths)
    return lax.cond(
        bound[0] <= (safe_exponent / exponent_scale) ** 2,
        lambda *_: out,
        any_size,
        queries,
        keys,
        values,
        doc_lengths,
    )


def solution(mesh):
    in_specs = (P(("ctx", "head"), None), P("ctx", "head"), P("ctx", "head"), P())
    out_specs = P(("ctx", "head"), None)
    return jax.shard_map(
        per_device, mesh=mesh, in_specs=in_specs, out_specs=out_specs, check_vma=False
    )
```

```python
import math

import jax
import jax.numpy as jnp
from jax import lax
from jax.experimental import pallas as pl
from jax.experimental.pallas import tpu as pltpu
from jax.sharding import PartitionSpec as P

neg_big = -1e30
block_keys = 512
MESH = pl.DeviceIdType.MESH

head_depth = 128
heads_per_group = 16
group_columns = heads_per_group * head_depth
own_tokens = 64
block = 256
row_keys = 4 * block
slot_columns = own_tokens * heads_per_group
exponent_scale = math.log2(math.e) / math.sqrt(head_depth)
safe_exponent = 100.0


def attend_kernel(
    q_ref,
    k_ref,
    v_ref,
    len_ref,
    out_ref,
    bound_ref,
    stage,
    keyval,
    q_in,
    q_cols,
    acc,
    denom,
    begins,
    o_part,
    stat_own,
    stat_in,
    stage_sem,
    chunk_sem,
    q_sem,
    o_sem,
    stat_sem,
    z_send,
    entry_send,
    x_send,
    y_send,
    q_send,
    sib_send,
    o_send,
    stat_send,
    own_sem,
):
    ctx = lax.axis_index("ctx")
    head = lax.axis_index("head")
    plane, y, x = ctx // 16, (ctx // 4) % 4, ctx % 4
    half, core = head // 2, head % 2
    yhi, xhi, ylo, xlo = y // 2, x // 2, y % 2, x % 2
    ybit, xbit = (ylo + yhi) % 2, (xlo + xhi) % 2
    group = ybit * 2 + xbit
    quad_row = plane * 4 + yhi * 2
    quad_pair = plane * 2 + yhi
    receiver = core == xbit
    same = (ybit == half).astype(jnp.int32)

    def ctx_of(p, yy, xx):
        return p * 16 + yy * 4 + xx

    sibling = (ctx, half * 2 + 1 - core)
    partners = [sibling, (ctx_of(plane, yhi * 2 + 1 - ylo, xhi * 2 + 1 - xlo), head)]
    for d in range(1, 4):
        partners.append((ctx_of(plane, y, (x + d) % 4), head))
        partners.append((ctx_of(plane, (y + d) % 4, x), head))
    for dz in range(1, 8):
        z = (half * 4 + plane + dz) % 8
        partners.append((ctx_of(z % 4, y, x), (z // 4) * 2 + core))
    barrier = pltpu.get_barrier_semaphore()
    for partner in partners:
        pl.semaphore_signal(barrier, inc=1, device_id=partner, device_id_type=MESH)

    mine = half * 4 + plane
    stage[mine, 0] = k_ref[...]
    v_t = v_ref[...].T
    stage[mine, 1] = jnp.concatenate([v_t[:, :128], v_t[:, 128:]], axis=0)
    own_slot = ylo * 2 + xlo

    lane = lax.broadcasted_iota(jnp.int32, (8, 128), 1) % own_tokens
    starts = []
    total = jnp.int32(0)
    for d in range(8):
        starts.append(total)
        total = total + len_ref[d]

    def slot_position(slot):
        c = ctx_of(plane, yhi * 2 + slot // 2, xhi * 2 + slot % 2)
        return c * block + head * own_tokens

    for slot in range(4):
        position = slot_position(slot) + lane
        begin = jnp.zeros((8, 128), jnp.int32)
        for start in starts:
            begin = jnp.maximum(begin, jnp.where(position >= start, start, 0))
        begins[slot] = begin

    acc[...] = jnp.zeros_like(acc)
    denom[...] = jnp.zeros_like(denom)
    own_keys = k_ref[...].astype(jnp.float32)
    key_norm = jnp.max(jnp.sum(own_keys * own_keys, axis=1))

    def columns_of(slot, read):
        best = jnp.zeros((1, 128), jnp.float32)
        for pair in range(8):
            two = read(pair)
            tile = jnp.concatenate([two[:, :128], two[:, 128:]], axis=0)
            turned = tile.astype(jnp.float32).T
            best = jnp.maximum(best, jnp.sum(turned * turned, axis=0, keepdims=True))
            at = pl.multiple_of(slot * slot_columns + pair * 128, 128)
            q_cols[:, pl.ds(at, 128)] = turned.astype(jnp.bfloat16)
        return best

    def read_own(pair):
        at = pl.multiple_of(group * group_columns + pair * 256, 128)
        return q_ref[:, pl.ds(at, 256)]

    query_norm = columns_of(own_slot, read_own)

    pl.semaphore_wait(barrier, len(partners))

    def remote(src, dst, send, recv, target):
        return pltpu.make_async_remote_copy(
            src_ref=src,
            dst_ref=dst,
            send_sem=send,
            recv_sem=recv,
            device_id=target,
            device_id_type=MESH,
        )

    def z_copy(n, index, to_half, to_plane):
        return remote(
            stage.at[index],
            stage.at[index],
            z_send.at[n],
            stage_sem.at[index],
            (ctx_of(to_plane, y, x), to_half * 2 + core),
        )

    def stage_index(flip, back):
        return ((half + flip) % 2) * 4 + plane - back

    z_hops = [
        (plane <= 3, 0, mine, 1 - half, jnp.minimum(plane + 1, 3)),
        (plane <= 2, 1, mine, half, plane + 1),
        (plane >= 1, 2, stage_index(1, 1), half, plane - 1),
        ((plane >= 1) & (plane <= 2), 3, stage_index(1, 1), half, plane + 1),
        ((plane >= 1) & (plane <= 2), 4, stage_index(0, 1), half, plane + 1),
    ]

    def z_start(n):
        pl.when(z_hops[n][0])(lambda: z_copy(*z_hops[n][1:]).start())

    def entry(flip, back, act):
        g = (half + flip) % 2
        p = plane - back
        index = stage_index(flip, back)
        to_y, to_x = yhi * 2 + (g + yhi) % 2, xhi * 2 + (core + xhi) % 2
        here = (to_y == y) & (to_x == x)
        pair = p * 2 + yhi
        target = keyval.at[pair, xhi, ylo, :, xlo]

        @pl.when((p >= 0) & jnp.logical_not(here))
        def _():
            copy = remote(
                stage.at[index],
                target,
                entry_send.at[flip * 3 + back],
                chunk_sem.at[pair * 2 + xhi],
                (ctx_of(plane, to_y, to_x), head),
            )
            copy.start() if act == "start" else copy.wait_send()

        if act == "start":

            @pl.when((p >= 0) & here)
            def _():
                pltpu.make_async_copy(
                    stage.at[index], target, chunk_sem.at[pair * 2 + xhi]
                ).start()

    def relay(flip, back, *hops):
        @pl.when(plane >= back)
        def _():
            z_copy(0, stage_index(flip, back), 1 - half, plane).wait_recv()

        for hop in hops:
            z_start(hop)
        entry(flip, back, "start")

    def mate(k):
        my, mx = (ylo + k // 2) % 2, (xlo + k % 2) % 2
        return my, mx

    def q_copy(k):
        my, mx = mate(k)
        to_group = ((my + yhi) % 2) * 2 + (mx + xhi) % 2
        columns = pl.ds(pl.multiple_of(to_group * group_columns, 128), group_columns)
        return remote(
            q_ref.at[:, columns],
            q_in.at[own_slot],
            q_send.at[k],
            q_sem.at[own_slot],
            (ctx_of(plane, yhi * 2 + my, xhi * 2 + mx), head),
        )

    def q_wait(k):
        my, mx = mate(k)
        slot = my * 2 + mx
        remote(q_in.at[slot], q_in.at[slot], q_send.at[0], q_sem.at[slot], sibling).wait_recv()

    middle = (plane == 1) | (plane == 2)
    pl.when(middle)(lambda: z_start(0))
    z_start(1)
    entry(0, 0, "start")
    for k in (1, 2, 3):
        q_copy(k).start()

    def chunk_copy(pair, side, send, target):
        chunk = keyval.at[pair, side]
        return remote(chunk, chunk, send, chunk_sem.at[pair * 2 + side], target)

    def sib_copy(pair, side):
        return chunk_copy(pair, side, sib_send.at[pair * 2 + side], sibling)

    x_next = (ctx_of(plane, y, (1 - xhi) * 2 + (xbit + 1 - xhi) % 2), head)
    y_next = (ctx_of(plane, (1 - yhi) * 2 + (ybit + 1 - yhi) % 2, x), head)

    def sent_on(back):
        return ((back == 0) & (yhi == 0)) | (back == 1) | ((back == 2) & (yhi == 1))

    def got_from(back):
        return ((back == 0) & (yhi == 1)) | (back == 1) | ((back == 2) & (yhi == 0))

    def x_copy(back):
        return chunk_copy((plane - back) * 2 + yhi, xhi, x_send.at[back], x_next)

    def y_copy(back, side):
        pair = (plane - back) * 2 + yhi
        return chunk_copy(pair, (xhi + side) % 2, y_send.at[back * 2 + side], y_next)

    def take_own(back):
        pair = (plane - back) * 2 + yhi

        @pl.when(plane >= back)
        def _():
            sib_copy(pair, xhi).wait_recv()

            @pl.when(receiver)
            def _():
                x_copy(back).start()
                sib_copy(pair, xhi).start()

    def pass_own(back):
        @pl.when((plane >= back) & receiver & sent_on(back))
        def _():
            y_copy(back, 0).start()

    def take_x(back):
        pair = (plane - back) * 2 + yhi

        @pl.when(plane >= back)
        def _():
            sib_copy(pair, 1 - xhi).wait_recv()

            @pl.when(receiver)
            def _():
                pl.when(sent_on(back))(lambda: y_copy(back, 1).start())
                sib_copy(pair, 1 - xhi).start()

    def take_y(back, side):
        pair = (plane - back) * 2 + 1 - yhi

        @pl.when((plane >= back) & got_from(back))
        def _():
            sib_copy(pair, (xhi + side) % 2).wait_recv()
            pl.when(receiver)(lambda: sib_copy(pair, (xhi + side) % 2).start())

    near_half = same == 1

    @pl.when(plane == 0)
    def _():
        z_copy(*z_hops[1][1:]).wait_send()
        z_start(0)

    relay(0, 1, 4)
    pl.when(plane == 3)(lambda: z_start(0))

    @pl.when(near_half & (yhi == 0))
    def _():
        take_own(0)
        pass_own(0)

    relay(1, 1, 2, 3)
    relay(0, 2)
    relay(1, 0)
    relay(1, 2)
    take_own(1)
    pass_own(1)

    def norms(query_norm):
        rank = lax.broadcasted_iota(jnp.int32, (8, 128), 0)
        return jnp.where(rank < 4, jnp.broadcast_to(query_norm, (8, 128)), key_norm)

    stat_own[0] = norms(query_norm)

    def slot_of(k):
        my, mx = mate(k)
        return my * 2 + mx

    def take_queries(k):
        q_wait(k)
        slot = slot_of(k)
        best = columns_of(slot, lambda pair: q_in[slot, :, pl.ds(pair * 256, 256)])
        stat_own[0] = jnp.maximum(stat_own[0], norms(best))

    rounds = [[(0, sibling)], [], [], []]
    for d in range(1, 4):
        rounds[1].append((d, (ctx_of(plane, y, (x + d) % 4), head)))
        rounds[2].append((3 + d, (ctx_of(plane, (y + d) % 4, x), head)))
    for dz in range(1, 8):
        z = (half * 4 + plane + dz) % 8
        rounds[3].append((6 + dz, (ctx_of(z % 4, y, x), (z // 4) * 2 + core)))

    def stat_copy(r, n, target):
        return remote(stat_own.at[r], stat_in.at[n], stat_send.at[n], stat_sem.at[n], target)

    def stat_start(r):
        for n, target in rounds[r]:
            stat_copy(r, n, target).start()

    def stat_finish(r):
        best = stat_own[r]
        for n, target in rounds[r]:
            stat_copy(r, n, target).wait()
            best = jnp.maximum(best, stat_in[n])
        stat_own[r + 1] = best

    key_rank = lax.broadcasted_iota(jnp.int32, (block, 128), 0)

    def absorb_keys(slot, keys, values_t, masks):
        columns = pl.ds(pl.multiple_of(slot * slot_columns, 128), slot_columns)
        scores = jnp.dot(keys, q_cols[:, columns], preferred_element_type=jnp.float32)
        visible = jnp.concatenate(masks, axis=0)
        visible = jnp.concatenate([visible] * (slot_columns // 128), axis=1)
        weights = jnp.where(visible, jnp.exp2(scores * exponent_scale), 0.0)
        ones = jnp.ones((8, values_t.shape[1]), jnp.bfloat16)
        sums = jnp.dot(
            jnp.concatenate([values_t, ones], axis=0),
            weights.astype(jnp.bfloat16),
            preferred_element_type=jnp.float32,
        )
        acc[:, columns] += sums[:head_depth]
        denom[:, columns] += sums[head_depth:]

    def key_block(row, i):
        return keyval[row // 2, i // 2, row % 2, 0, i % 2]

    def value_block(row, i):
        tile = keyval[row // 2, i // 2, row % 2, 1, i % 2]
        return jnp.concatenate([tile[:128], tile[128:]], axis=1)

    def whole_blocks(slot, blocks):
        begin = begins[slot][:1]
        absorb_keys(
            slot,
            jnp.concatenate([key_block(row, i) for row, i in blocks], axis=0),
            jnp.concatenate([value_block(row, i) for row, i in blocks], axis=1),
            [key_rank + (row * row_keys + i * block) >= begin for row, i in blocks],
        )

    def full_row(row, slot):
        whole_blocks(slot, [(row, i) for i in range(4)])

    def full_chunk(pair, side, slot):
        blocks = [(pair * 2 + dy, side * 2 + dx) for dy in range(2) for dx in range(2)]
        whole_blocks(slot, blocks)

    def edge_rows(slot):
        slot_y, slot_x = yhi * 2 + slot // 2, xhi * 2 + slot % 2
        near = plane * 4 + slot_y
        far = near - 8
        there = (far >= 0).astype(jnp.int32)
        held = there * far + (1 - there) * near
        begin = begins[slot][:1]
        position = slot_position(slot) + lane[:1]
        keys, values_t, masks = [], [], []
        for i in range(4):
            is_near = (slot_x >= i).astype(jnp.int32)
            row = is_near * near + (1 - is_near) * held
            first = (is_near * near + (1 - is_near) * far) * row_keys + i * block
            keys.append(key_block(row, i))
            values_t.append(value_block(row, i))
            key = key_rank + first
            masks.append((key >= begin) & (key <= position))
        absorb_keys(slot, jnp.concatenate(keys, axis=0), jnp.concatenate(values_t, axis=1), masks)

        @pl.when(far >= 0)
        def _():
            first = far * row_keys + slot_x * block
            absorb_keys(
                slot,
                key_block(held, slot_x),
                value_block(held, slot_x),
                [key_rank + first >= begin],
            )

    def when_near(act, near):
        pl.when(same == near)(act)

    far_steps = {('own', 'first'): 4, ('x', 1): 4, ('y', 1, 0): 7, ('own', 'second'): 8, ('pass', 'first'): 9, ('y', 1, 1): 11, ('x', 'first'): 12, ('x', 'second'): 15, ('y', 'second', 0): 17}
    near_steps = {('own', 'first'): 2, ('pass', 'first'): 2, ('x', 1): 3, ('own', 'second'): 5, ('x', 'first'): 7, ('y', 1, 0): 7, ('y', 1, 1): 10, ('x', 'second'): 11, ('y', 'second', 0): 16}
    stat_steps = [5, 8, 12, 15]
    events = []
    for key, at in far_steps.items():
        events.append((at, 0, key))
    for key, at in near_steps.items():
        events.append((at, 1, key))

    def act_on(key):
        kind, back = key[0], key[1]
        if back == "first":
            back = 2 * yhi
        elif back == "second":
            back = 2 - 2 * yhi
        if kind == "relay":
            relay(1, back)
        elif kind == "own":
            early = (same == 1) & (yhi == 0) & (back == 0)
            pl.when(jnp.logical_not(early))(lambda: take_own(back))
        elif kind == "pass":
            early = (same == 1) & (yhi == 0) & (back == 0)
            pl.when(jnp.logical_not(early))(lambda: pass_own(back))
        elif kind == "x":
            take_x(back)
        else:
            take_y(back, key[2])

    def before(step, at):
        here = [(near, key) for when, near, key in events if when == at]
        starts_here = [r for r in range(4) if stat_steps[r] == at]
        if here or starts_here or 1 <= at <= 3:

            @pl.when(step == at)
            def _():
                if 1 <= at <= 3:
                    take_queries(at)
                for near, key in here:
                    when_near(lambda key=key: act_on(key), near)
                for r in starts_here:
                    if r:
                        stat_finish(r - 1)
                    stat_start(r)

    first_y = yhi * -3 + (1 - yhi) * -1

    def chunk_step(chunk, k):
        side = (xhi + chunk) % 2
        order = chunk // 2
        back = jnp.where(order == 0, -2, jnp.where(order == 1, first_y, -4 - first_y))
        pair = quad_pair + back

        @pl.when(pair >= 0)
        def _():
            full_chunk(pair, side, slot_of(k))

    @pl.loop(0, 16)
    def _(step):
        for at in range(16):
            before(step, at)
        chunk_step(step // 4, step % 4)

    def edge_step(slot):
        last = quad_row - 7 * (1 - slot // 2)

        @pl.when(last >= 0)
        def _():
            full_row(last, slot)

        edge_rows(slot)

    @pl.loop(16, 18)
    def _(step):
        for at in range(16, 18):
            before(step, at)
        edge_step(slot_of(19 - step))

    act_on(("y", "second", 1))

    def o_columns():
        return pl.ds(pl.multiple_of(group * group_columns, 128), group_columns)

    def o_copy(k):
        my, mx = mate(k)
        return remote(
            o_part.at[my * 2 + mx],
            out_ref.at[:, o_columns()],
            o_send.at[k],
            o_sem.at[k],
            (ctx_of(plane, yhi * 2 + my, xhi * 2 + mx), head),
        )

    def o_arrival(k):
        my, mx = mate(k)
        from_group = ((my + yhi) % 2) * 2 + (mx + xhi) % 2
        columns = pl.ds(pl.multiple_of(from_group * group_columns, 128), group_columns)
        return remote(
            o_part.at[own_slot], out_ref.at[:, columns], o_send.at[k], o_sem.at[k], sibling
        )

    @pl.loop(0, 4)
    def _(turn):
        k = 3 - turn
        slot = slot_of(k)
        pl.when(turn >= 2)(lambda: edge_step(slot))

        @pl.loop(4, 6)
        def _(chunk):
            chunk_step(chunk, k)

        for pair in range(8):
            columns = pl.ds(pl.multiple_of(slot * slot_columns + pair * 128, 128), 128)
            share = acc[:, columns] / denom[:1, columns]
            back = share.T.astype(jnp.bfloat16)
            o_part[slot, :, pl.ds(pair * 256, 128)] = back[:own_tokens]
            o_part[slot, :, pl.ds(pair * 256 + 128, 128)] = back[own_tokens:]
        pl.when(k > 0)(lambda: o_copy(k).start())

    home = pltpu.make_async_copy(o_part.at[own_slot], out_ref.at[:, o_columns()], own_sem)
    home.start()
    stat_finish(3)
    bound_ref[0] = jnp.max(stat_own[4, :4]) * jnp.max(stat_own[4, 4:])

    for k in (1, 2, 3):
        q_copy(k).wait_send()
    for n, hop in enumerate(z_hops):
        left = hop[0] & (plane > 0) if n == 1 else hop[0]
        pl.when(left)(lambda hop=hop: z_copy(*hop[1:]).wait_send())
    for flip in range(2):
        for back in range(3):
            entry(flip, back, "wait")
    for back in range(3):

        @pl.when((plane >= back) & receiver)
        def _():
            x_copy(back).wait_send()
            sib_copy((plane - back) * 2 + yhi, 0).wait_send()
            sib_copy((plane - back) * 2 + yhi, 1).wait_send()

            @pl.when(sent_on(back))
            def _():
                y_copy(back, 0).wait_send()
                y_copy(back, 1).wait_send()

            @pl.when(got_from(back))
            def _():
                sib_copy((plane - back) * 2 + 1 - yhi, 0).wait_send()
                sib_copy((plane - back) * 2 + 1 - yhi, 1).wait_send()

    for k in (3, 2, 1):
        o_copy(k).wait_send()
        o_arrival(k).wait_recv()
    home.wait()


def attend(queries, keys, values, doc_lengths):
    vmem = pl.BlockSpec(memory_space=pltpu.VMEM)
    smem = pl.BlockSpec(memory_space=pltpu.SMEM)
    elements = 9 * row_keys * 4 * slot_columns
    dma = pltpu.SemaphoreType.DMA
    return pl.pallas_call(
        attend_kernel,
        name="attend",
        out_shape=(
            jax.ShapeDtypeStruct(queries.shape, jnp.bfloat16),
            jax.ShapeDtypeStruct((1,), jnp.float32),
        ),
        in_specs=[vmem, vmem, vmem, smem],
        out_specs=(vmem, smem),
        scratch_shapes=[
            pltpu.VMEM((8, 2, block, head_depth), jnp.bfloat16),
            pltpu.VMEM((8, 2, 2, 2, 2, block, head_depth), jnp.bfloat16),
            pltpu.VMEM((4, own_tokens, group_columns), jnp.bfloat16),
            pltpu.VMEM((head_depth, 4 * slot_columns), jnp.bfloat16),
            pltpu.VMEM((head_depth, 4 * slot_columns), jnp.float32),
            pltpu.VMEM((8, 4 * slot_columns), jnp.float32),
            pltpu.VMEM((4, 8, 128), jnp.int32),
            pltpu.VMEM((4, own_tokens, group_columns), jnp.bfloat16),
            pltpu.VMEM((5, 8, 128), jnp.float32),
            pltpu.VMEM((14, 8, 128), jnp.float32),
            dma((8,)),
            dma((16,)),
            dma((4,)),
            dma((4,)),
            dma((14,)),
            dma((5,)),
            dma((6,)),
            dma((3,)),
            dma((6,)),
            dma((4,)),
            dma((16,)),
            dma((4,)),
            dma((14,)),
            dma,
        ],
        compiler_params=pltpu.CompilerParams(
            collective_id=0, has_side_effects=True, vmem_limit_bytes=56 << 20
        ),
        cost_estimate=pl.CostEstimate(
            flops=4 * elements * head_depth, bytes_accessed=4 << 20, transcendentals=elements
        ),
    )(queries, keys, values, doc_lengths)


def token_begins(doc_starts, positions):
    hit = doc_starts[None, :] <= positions[:, None]
    return jnp.max(jnp.where(hit, doc_starts[None, :], 0), axis=1)


def absorb(
    carried, held_tiles, tile_starts, doc_starts, key_piece, value_piece, piece_start, tok_rows
):
    top_scores, denominators, runnings = carried
    piece_rows = key_piece.shape[0]
    block_width = math.gcd(piece_rows, block_keys)
    tile_count, query_rows, head_depth = held_tiles.shape
    group_size = query_rows // tok_rows
    score_scale = 1.0 / math.sqrt(head_depth)
    new_tops, new_denoms, new_runs = ([], [], [])
    for tile_num in range(tile_count):
        tile_start = tile_starts[tile_num]
        positions = tile_start + jnp.arange(tok_rows, dtype=jnp.int32)
        begins = token_begins(doc_starts, positions)
        low_pos = jnp.maximum(begins[0], piece_start)
        high_pos = jnp.minimum(tile_start + tok_rows, piece_start + piece_rows)
        first_block = low_pos // block_width
        last_block = jnp.maximum(first_block, (high_pos + block_width - 1) // block_width)
        tile_query = held_tiles[tile_num]

        def add_block(block_index, loop_state):
            top_score, denominator, running = loop_state
            offset = block_index * block_width
            key_block = lax.dynamic_slice_in_dim(key_piece, offset, block_width, 0)
            value_block = lax.dynamic_slice_in_dim(value_piece, offset, block_width, 0)
            scores = (
                lax.dot_general(
                    tile_query,
                    key_block,
                    (((1,), (1,)), ((), ())),
                    preferred_element_type=jnp.float32,
                )
                * score_scale
            )
            key_pos = offset + jnp.arange(block_width, dtype=jnp.int32)
            visible = (key_pos[None, :] <= positions[:, None]) & (
                key_pos[None, :] >= begins[:, None]
            )
            visible = jnp.repeat(visible, group_size, axis=0)
            new_top = jnp.maximum(top_score, jnp.max(jnp.where(visible, scores, neg_big), axis=1))
            weights = jnp.where(visible, jnp.exp(scores - new_top[:, None]), 0.0)
            rescale = jnp.exp(top_score - new_top)
            denominator = denominator * rescale + jnp.sum(weights, axis=1)
            running = running * rescale[:, None] + jnp.dot(
                weights.astype(jnp.bfloat16), value_block, preferred_element_type=jnp.float32
            )
            return (new_top, denominator, running)

        result = lax.fori_loop(
            first_block,
            last_block,
            add_block,
            (top_scores[tile_num], denominators[tile_num], runnings[tile_num]),
        )
        new_tops.append(result[0])
        new_denoms.append(result[1])
        new_runs.append(result[2])
    return (jnp.stack(new_tops), jnp.stack(new_denoms), jnp.stack(new_runs))


def from_all(piece):
    copies = jnp.tile(piece, (lax.axis_size("ctx"), 1))
    return lax.all_to_all(copies, "ctx", split_axis=0, concat_axis=0, tiled=True)


def any_size(queries, keys, values, doc_lengths):
    by_head = lax.all_to_all(queries, "head", split_axis=1, concat_axis=0, tiled=True)
    tok_dev = by_head.shape[0]
    head_depth = keys.shape[1]
    group_size = by_head.shape[1] // head_depth
    tile_count = 8
    tok_rows = tok_dev // tile_count
    shard_index = lax.axis_index("ctx")
    doc_starts = jnp.cumsum(doc_lengths) - doc_lengths
    tile_query = by_head.reshape(tile_count, tok_rows * group_size, head_depth)
    tile_starts = shard_index * tok_dev + jnp.arange(tile_count, dtype=jnp.int32) * tok_rows
    query_rows = tok_rows * group_size
    initial = (
        jnp.full((tile_count, query_rows), neg_big, jnp.float32),
        jnp.zeros((tile_count, query_rows), jnp.float32),
        jnp.zeros((tile_count, query_rows, head_depth), jnp.float32),
    )
    whole_keys, whole_values = (
        from_all(keys),
        from_all(values),
    )
    carried = absorb(
        initial,
        tile_query,
        tile_starts,
        doc_starts,
        whole_keys,
        whole_values,
        jnp.int32(0),
        tok_rows,
    )
    results = (carried[2] / carried[1][..., None]).astype(jnp.bfloat16)
    merged = results.reshape(tok_dev, group_size * head_depth)
    return lax.all_to_all(merged, "head", split_axis=0, concat_axis=1, tiled=True)


def per_device(queries, keys, values, doc_lengths):
    out, bound = attend(queries, keys, values, doc_lengths)
    return lax.cond(
        bound[0] <= (safe_exponent / exponent_scale) ** 2,
        lambda *_: out,
        any_size,
        queries,
        keys,
        values,
        doc_lengths,
    )


def solution(mesh):
    in_specs = (P(("ctx", "head"), None), P("ctx", "head"), P("ctx", "head"), P())
    out_specs = P(("ctx", "head"), None)
    return jax.shard_map(
        per_device, mesh=mesh, in_specs=in_specs, out_specs=out_specs, check_vma=False
    )
```

```python
import math

import jax
import jax.numpy as jnp
from jax import lax
from jax.experimental import pallas as pl
from jax.experimental.pallas import tpu as pltpu
from jax.sharding import PartitionSpec as P

neg_big = -1e30
block_keys = 512
MESH = pl.DeviceIdType.MESH

head_depth = 128
heads_per_group = 16
group_columns = heads_per_group * head_depth
own_tokens = 64
block = 256
row_keys = 4 * block
slot_columns = own_tokens * heads_per_group
exponent_scale = math.log2(math.e) / math.sqrt(head_depth)
safe_exponent = 100.0


def attend_kernel(
    q_ref,
    k_ref,
    v_ref,
    len_ref,
    out_ref,
    bound_ref,
    stage,
    keyval,
    q_in,
    q_cols,
    acc,
    denom,
    begins,
    o_part,
    stat_own,
    stat_in,
    stage_sem,
    chunk_sem,
    q_sem,
    o_sem,
    stat_sem,
    z_send,
    entry_send,
    x_send,
    y_send,
    q_send,
    sib_send,
    o_send,
    stat_send,
    own_sem,
):
    ctx = lax.axis_index("ctx")
    head = lax.axis_index("head")
    plane, y, x = ctx // 16, (ctx // 4) % 4, ctx % 4
    half, core = head // 2, head % 2
    yhi, xhi, ylo, xlo = y // 2, x // 2, y % 2, x % 2
    ybit, xbit = (ylo + yhi) % 2, (xlo + xhi) % 2
    group = ybit * 2 + xbit
    quad_row = plane * 4 + yhi * 2
    quad_pair = plane * 2 + yhi
    receiver = core == xbit
    same = (ybit == half).astype(jnp.int32)

    def ctx_of(p, yy, xx):
        return p * 16 + yy * 4 + xx

    sibling = (ctx, half * 2 + 1 - core)
    partners = [sibling, (ctx_of(plane, yhi * 2 + 1 - ylo, xhi * 2 + 1 - xlo), head)]
    for d in range(1, 4):
        partners.append((ctx_of(plane, y, (x + d) % 4), head))
        partners.append((ctx_of(plane, (y + d) % 4, x), head))
    for dz in range(1, 8):
        z = (half * 4 + plane + dz) % 8
        partners.append((ctx_of(z % 4, y, x), (z // 4) * 2 + core))
    barrier = pltpu.get_barrier_semaphore()
    for partner in partners:
        pl.semaphore_signal(barrier, inc=1, device_id=partner, device_id_type=MESH)

    mine = half * 4 + plane
    stage[mine, 0] = k_ref[...]
    v_t = v_ref[...].T
    stage[mine, 1] = jnp.concatenate([v_t[:, :128], v_t[:, 128:]], axis=0)
    own_slot = ylo * 2 + xlo

    lane = lax.broadcasted_iota(jnp.int32, (8, 128), 1) % own_tokens
    starts = []
    total = jnp.int32(0)
    for d in range(8):
        starts.append(total)
        total = total + len_ref[d]

    def slot_position(slot):
        c = ctx_of(plane, yhi * 2 + slot // 2, xhi * 2 + slot % 2)
        return c * block + head * own_tokens

    for slot in range(4):
        position = slot_position(slot) + lane
        begin = jnp.zeros((8, 128), jnp.int32)
        for start in starts:
            begin = jnp.maximum(begin, jnp.where(position >= start, start, 0))
        begins[slot] = begin

    acc[...] = jnp.zeros_like(acc)
    denom[...] = jnp.zeros_like(denom)
    own_keys = k_ref[...].astype(jnp.float32)
    key_norm = jnp.max(jnp.sum(own_keys * own_keys, axis=1))

    def columns_of(slot, read):
        best = jnp.zeros((1, 128), jnp.float32)
        for pair in range(8):
            two = read(pair)
            tile = jnp.concatenate([two[:, :128], two[:, 128:]], axis=0)
            turned = tile.astype(jnp.float32).T
            best = jnp.maximum(best, jnp.sum(turned * turned, axis=0, keepdims=True))
            at = pl.multiple_of(slot * slot_columns + pair * 128, 128)
            q_cols[:, pl.ds(at, 128)] = turned.astype(jnp.bfloat16)
        return best

    def read_own(pair):
        at = pl.multiple_of(group * group_columns + pair * 256, 128)
        return q_ref[:, pl.ds(at, 256)]

    query_norm = columns_of(own_slot, read_own)

    pl.semaphore_wait(barrier, len(partners))

    def remote(src, dst, send, recv, target):
        return pltpu.make_async_remote_copy(
            src_ref=src,
            dst_ref=dst,
            send_sem=send,
            recv_sem=recv,
            device_id=target,
            device_id_type=MESH,
        )

    def z_copy(n, index, to_half, to_plane):
        return remote(
            stage.at[index],
            stage.at[index],
            z_send.at[n],
            stage_sem.at[index],
            (ctx_of(to_plane, y, x), to_half * 2 + core),
        )

    def stage_index(flip, back):
        return ((half + flip) % 2) * 4 + plane - back

    z_hops = [
        (plane <= 3, 0, mine, 1 - half, jnp.minimum(plane + 1, 3)),
        (plane <= 2, 1, mine, half, plane + 1),
        (plane >= 1, 2, stage_index(1, 1), half, plane - 1),
        ((plane >= 1) & (plane <= 2), 3, stage_index(1, 1), half, plane + 1),
        ((plane >= 1) & (plane <= 2), 4, stage_index(0, 1), half, plane + 1),
    ]

    def z_start(n):
        pl.when(z_hops[n][0])(lambda: z_copy(*z_hops[n][1:]).start())

    def entry(flip, back, act):
        g = (half + flip) % 2
        p = plane - back
        index = stage_index(flip, back)
        to_y, to_x = yhi * 2 + (g + yhi) % 2, xhi * 2 + (core + xhi) % 2
        here = (to_y == y) & (to_x == x)
        pair = p * 2 + yhi
        target = keyval.at[pair, xhi, ylo, :, xlo]

        @pl.when((p >= 0) & jnp.logical_not(here))
        def _():
            copy = remote(
                stage.at[index],
                target,
                entry_send.at[flip * 3 + back],
                chunk_sem.at[pair * 2 + xhi],
                (ctx_of(plane, to_y, to_x), head),
            )
            copy.start() if act == "start" else copy.wait_send()

        if act == "start":

            @pl.when((p >= 0) & here)
            def _():
                pltpu.make_async_copy(
                    stage.at[index], target, chunk_sem.at[pair * 2 + xhi]
                ).start()

    def relay(flip, back, *hops):
        @pl.when(plane >= back)
        def _():
            z_copy(0, stage_index(flip, back), 1 - half, plane).wait_recv()

        for hop in hops:
            z_start(hop)
        entry(flip, back, "start")

    def mate(k):
        my, mx = (ylo + k // 2) % 2, (xlo + k % 2) % 2
        return my, mx

    def q_copy(k):
        my, mx = mate(k)
        to_group = ((my + yhi) % 2) * 2 + (mx + xhi) % 2
        columns = pl.ds(pl.multiple_of(to_group * group_columns, 128), group_columns)
        return remote(
            q_ref.at[:, columns],
            q_in.at[own_slot],
            q_send.at[k],
            q_sem.at[own_slot],
            (ctx_of(plane, yhi * 2 + my, xhi * 2 + mx), head),
        )

    def q_wait(k):
        my, mx = mate(k)
        slot = my * 2 + mx
        remote(q_in.at[slot], q_in.at[slot], q_send.at[0], q_sem.at[slot], sibling).wait_recv()

    middle = (plane == 1) | (plane == 2)
    pl.when(middle)(lambda: z_start(0))
    z_start(1)
    entry(0, 0, "start")
    for k in (1, 2, 3):
        q_copy(k).start()

    def chunk_copy(pair, side, send, target):
        chunk = keyval.at[pair, side]
        return remote(chunk, chunk, send, chunk_sem.at[pair * 2 + side], target)

    def sib_copy(pair, side):
        return chunk_copy(pair, side, sib_send.at[pair * 2 + side], sibling)

    x_next = (ctx_of(plane, y, (1 - xhi) * 2 + (xbit + 1 - xhi) % 2), head)
    y_next = (ctx_of(plane, (1 - yhi) * 2 + (ybit + 1 - yhi) % 2, x), head)

    def sent_on(back):
        return ((back == 0) & (yhi == 0)) | (back == 1) | ((back == 2) & (yhi == 1))

    def got_from(back):
        return ((back == 0) & (yhi == 1)) | (back == 1) | ((back == 2) & (yhi == 0))

    def x_copy(back):
        return chunk_copy((plane - back) * 2 + yhi, xhi, x_send.at[back], x_next)

    def y_copy(back, side):
        pair = (plane - back) * 2 + yhi
        return chunk_copy(pair, (xhi + side) % 2, y_send.at[back * 2 + side], y_next)

    def take_own(back):
        pair = (plane - back) * 2 + yhi

        @pl.when(plane >= back)
        def _():
            sib_copy(pair, xhi).wait_recv()

            @pl.when(receiver)
            def _():
                x_copy(back).start()
                sib_copy(pair, xhi).start()

    def pass_own(back):
        @pl.when((plane >= back) & receiver & sent_on(back))
        def _():
            y_copy(back, 0).start()

    def take_x(back):
        pair = (plane - back) * 2 + yhi

        @pl.when(plane >= back)
        def _():
            sib_copy(pair, 1 - xhi).wait_recv()

            @pl.when(receiver)
            def _():
                pl.when(sent_on(back))(lambda: y_copy(back, 1).start())
                sib_copy(pair, 1 - xhi).start()

    def take_y(back, side):
        pair = (plane - back) * 2 + 1 - yhi

        @pl.when((plane >= back) & got_from(back))
        def _():
            sib_copy(pair, (xhi + side) % 2).wait_recv()
            pl.when(receiver)(lambda: sib_copy(pair, (xhi + side) % 2).start())

    near_half = same == 1

    @pl.when(plane == 0)
    def _():
        z_copy(*z_hops[1][1:]).wait_send()
        z_start(0)

    relay(0, 1, 4)
    pl.when(plane == 3)(lambda: z_start(0))

    @pl.when(near_half & (yhi == 0))
    def _():
        take_own(0)
        pass_own(0)

    relay(1, 1, 2, 3)
    relay(0, 2)
    relay(1, 0)
    relay(1, 2)
    take_own(1)
    pass_own(1)

    def norms(query_norm):
        rank = lax.broadcasted_iota(jnp.int32, (8, 128), 0)
        return jnp.where(rank < 4, jnp.broadcast_to(query_norm, (8, 128)), key_norm)

    stat_own[0] = norms(query_norm)

    def slot_of(k):
        my, mx = mate(k)
        return my * 2 + mx

    def take_queries(k):
        q_wait(k)
        slot = slot_of(k)
        best = columns_of(slot, lambda pair: q_in[slot, :, pl.ds(pair * 256, 256)])
        stat_own[0] = jnp.maximum(stat_own[0], norms(best))

    rounds = [[(0, sibling)], [], [], []]
    for d in range(1, 4):
        rounds[1].append((d, (ctx_of(plane, y, (x + d) % 4), head)))
        rounds[2].append((3 + d, (ctx_of(plane, (y + d) % 4, x), head)))
    for dz in range(1, 8):
        z = (half * 4 + plane + dz) % 8
        rounds[3].append((6 + dz, (ctx_of(z % 4, y, x), (z // 4) * 2 + core)))

    def stat_copy(r, n, target):
        return remote(stat_own.at[r], stat_in.at[n], stat_send.at[n], stat_sem.at[n], target)

    def stat_start(r):
        for n, target in rounds[r]:
            stat_copy(r, n, target).start()

    def stat_finish(r):
        best = stat_own[r]
        for n, target in rounds[r]:
            stat_copy(r, n, target).wait()
            best = jnp.maximum(best, stat_in[n])
        stat_own[r + 1] = best

    key_rank = lax.broadcasted_iota(jnp.int32, (block, 128), 0)

    def absorb_keys(slot, keys, values_t, masks):
        columns = pl.ds(pl.multiple_of(slot * slot_columns, 128), slot_columns)
        scores = jnp.dot(keys, q_cols[:, columns], preferred_element_type=jnp.float32)
        visible = jnp.concatenate(masks, axis=0)
        visible = jnp.concatenate([visible] * (slot_columns // 128), axis=1)
        weights = jnp.where(visible, jnp.exp2(scores * exponent_scale), 0.0)
        ones = jnp.ones((8, values_t.shape[1]), jnp.bfloat16)
        sums = jnp.dot(
            jnp.concatenate([values_t, ones], axis=0),
            weights.astype(jnp.bfloat16),
            preferred_element_type=jnp.float32,
        )
        acc[:, columns] += sums[:head_depth]
        denom[:, columns] += sums[head_depth:]

    def key_block(row, i):
        return keyval[row // 2, i // 2, row % 2, 0, i % 2]

    def value_block(row, i):
        tile = keyval[row // 2, i // 2, row % 2, 1, i % 2]
        return jnp.concatenate([tile[:128], tile[128:]], axis=1)

    def whole_blocks(slot, blocks):
        begin = begins[slot][:1]
        absorb_keys(
            slot,
            jnp.concatenate([key_block(row, i) for row, i in blocks], axis=0),
            jnp.concatenate([value_block(row, i) for row, i in blocks], axis=1),
            [key_rank + (row * row_keys + i * block) >= begin for row, i in blocks],
        )

    def full_row(row, slot):
        whole_blocks(slot, [(row, i) for i in range(4)])

    def full_chunk(pair, side, slot):
        blocks = [(pair * 2 + dy, side * 2 + dx) for dy in range(2) for dx in range(2)]
        whole_blocks(slot, blocks)

    def edge_rows(slot):
        slot_y, slot_x = yhi * 2 + slot // 2, xhi * 2 + slot % 2
        near = plane * 4 + slot_y
        far = near - 8
        there = (far >= 0).astype(jnp.int32)
        held = there * far + (1 - there) * near
        begin = begins[slot][:1]
        position = slot_position(slot) + lane[:1]
        keys, values_t, masks = [], [], []
        for i in range(4):
            is_near = (slot_x >= i).astype(jnp.int32)
            row = is_near * near + (1 - is_near) * held
            first = (is_near * near + (1 - is_near) * far) * row_keys + i * block
            keys.append(key_block(row, i))
            values_t.append(value_block(row, i))
            key = key_rank + first
            masks.append((key >= begin) & (key <= position))
        absorb_keys(slot, jnp.concatenate(keys, axis=0), jnp.concatenate(values_t, axis=1), masks)

        @pl.when(far >= 0)
        def _():
            first = far * row_keys + slot_x * block
            absorb_keys(
                slot,
                key_block(held, slot_x),
                value_block(held, slot_x),
                [key_rank + first >= begin],
            )

    def when_near(act, near):
        pl.when(same == near)(act)

    far_steps = {('own', 'first'): 4, ('x', 1): 4, ('y', 1, 0): 7, ('own', 'second'): 8, ('pass', 'first'): 9, ('y', 1, 1): 11, ('x', 'first'): 12, ('x', 'second'): 15, ('y', 'second', 0): 17}
    near_steps = {('own', 'first'): 2, ('pass', 'first'): 2, ('x', 1): 3, ('own', 'second'): 5, ('x', 'first'): 7, ('y', 1, 0): 7, ('y', 1, 1): 10, ('x', 'second'): 11, ('y', 'second', 0): 16}
    stat_steps = [9, 12, 15, 17]
    events = []
    for key, at in far_steps.items():
        events.append((at, 0, key))
    for key, at in near_steps.items():
        events.append((at, 1, key))

    def act_on(key):
        kind, back = key[0], key[1]
        if back == "first":
            back = 2 * yhi
        elif back == "second":
            back = 2 - 2 * yhi
        if kind == "relay":
            relay(1, back)
        elif kind == "own":
            early = (same == 1) & (yhi == 0) & (back == 0)
            pl.when(jnp.logical_not(early))(lambda: take_own(back))
        elif kind == "pass":
            early = (same == 1) & (yhi == 0) & (back == 0)
            pl.when(jnp.logical_not(early))(lambda: pass_own(back))
        elif kind == "x":
            take_x(back)
        else:
            take_y(back, key[2])

    def before(step, at):
        here = [(near, key) for when, near, key in events if when == at]
        starts_here = [r for r in range(4) if stat_steps[r] == at]
        if here or starts_here or 1 <= at <= 3:

            @pl.when(step == at)
            def _():
                if 1 <= at <= 3:
                    take_queries(at)
                for near, key in here:
                    when_near(lambda key=key: act_on(key), near)
                for r in starts_here:
                    if r:
                        stat_finish(r - 1)
                    stat_start(r)

    first_y = yhi * -3 + (1 - yhi) * -1

    def chunk_step(chunk, k):
        side = (xhi + chunk) % 2
        order = chunk // 2
        back = jnp.where(order == 0, -2, jnp.where(order == 1, first_y, -4 - first_y))
        pair = quad_pair + back

        @pl.when(pair >= 0)
        def _():
            full_chunk(pair, side, slot_of(k))

    @pl.loop(0, 16)
    def _(step):
        for at in range(16):
            before(step, at)
        chunk_step(step // 4, step % 4)

    def edge_step(slot):
        last = quad_row - 7 * (1 - slot // 2)

        @pl.when(last >= 0)
        def _():
            full_row(last, slot)

        edge_rows(slot)

    @pl.loop(16, 18)
    def _(step):
        for at in range(16, 18):
            before(step, at)
        edge_step(slot_of(19 - step))

    act_on(("y", "second", 1))

    def o_columns():
        return pl.ds(pl.multiple_of(group * group_columns, 128), group_columns)

    def o_copy(k):
        my, mx = mate(k)
        return remote(
            o_part.at[my * 2 + mx],
            out_ref.at[:, o_columns()],
            o_send.at[k],
            o_sem.at[k],
            (ctx_of(plane, yhi * 2 + my, xhi * 2 + mx), head),
        )

    def o_arrival(k):
        my, mx = mate(k)
        from_group = ((my + yhi) % 2) * 2 + (mx + xhi) % 2
        columns = pl.ds(pl.multiple_of(from_group * group_columns, 128), group_columns)
        return remote(
            o_part.at[own_slot], out_ref.at[:, columns], o_send.at[k], o_sem.at[k], sibling
        )

    @pl.loop(0, 4)
    def _(turn):
        k = 3 - turn
        slot = slot_of(k)
        pl.when(turn >= 2)(lambda: edge_step(slot))

        @pl.loop(4, 6)
        def _(chunk):
            chunk_step(chunk, k)

        for pair in range(8):
            columns = pl.ds(pl.multiple_of(slot * slot_columns + pair * 128, 128), 128)
            share = acc[:, columns] / denom[:1, columns]
            back = share.T.astype(jnp.bfloat16)
            o_part[slot, :, pl.ds(pair * 256, 128)] = back[:own_tokens]
            o_part[slot, :, pl.ds(pair * 256 + 128, 128)] = back[own_tokens:]
        pl.when(k > 0)(lambda: o_copy(k).start())

    home = pltpu.make_async_copy(o_part.at[own_slot], out_ref.at[:, o_columns()], own_sem)
    home.start()
    stat_finish(3)
    bound_ref[0] = jnp.max(stat_own[4, :4]) * jnp.max(stat_own[4, 4:])

    for k in (1, 2, 3):
        q_copy(k).wait_send()
    for n, hop in enumerate(z_hops):
        left = hop[0] & (plane > 0) if n == 1 else hop[0]
        pl.when(left)(lambda hop=hop: z_copy(*hop[1:]).wait_send())
    for flip in range(2):
        for back in range(3):
            entry(flip, back, "wait")
    for back in range(3):

        @pl.when((plane >= back) & receiver)
        def _():
            x_copy(back).wait_send()
            sib_copy((plane - back) * 2 + yhi, 0).wait_send()
            sib_copy((plane - back) * 2 + yhi, 1).wait_send()

            @pl.when(sent_on(back))
            def _():
                y_copy(back, 0).wait_send()
                y_copy(back, 1).wait_send()

            @pl.when(got_from(back))
            def _():
                sib_copy((plane - back) * 2 + 1 - yhi, 0).wait_send()
                sib_copy((plane - back) * 2 + 1 - yhi, 1).wait_send()

    for k in (3, 2, 1):
        o_copy(k).wait_send()
        o_arrival(k).wait_recv()
    home.wait()


def attend(queries, keys, values, doc_lengths):
    vmem = pl.BlockSpec(memory_space=pltpu.VMEM)
    smem = pl.BlockSpec(memory_space=pltpu.SMEM)
    elements = 9 * row_keys * 4 * slot_columns
    dma = pltpu.SemaphoreType.DMA
    return pl.pallas_call(
        attend_kernel,
        name="attend",
        out_shape=(
            jax.ShapeDtypeStruct(queries.shape, jnp.bfloat16),
            jax.ShapeDtypeStruct((1,), jnp.float32),
        ),
        in_specs=[vmem, vmem, vmem, smem],
        out_specs=(vmem, smem),
        scratch_shapes=[
            pltpu.VMEM((8, 2, block, head_depth), jnp.bfloat16),
            pltpu.VMEM((8, 2, 2, 2, 2, block, head_depth), jnp.bfloat16),
            pltpu.VMEM((4, own_tokens, group_columns), jnp.bfloat16),
            pltpu.VMEM((head_depth, 4 * slot_columns), jnp.bfloat16),
            pltpu.VMEM((head_depth, 4 * slot_columns), jnp.float32),
            pltpu.VMEM((8, 4 * slot_columns), jnp.float32),
            pltpu.VMEM((4, 8, 128), jnp.int32),
            pltpu.VMEM((4, own_tokens, group_columns), jnp.bfloat16),
            pltpu.VMEM((5, 8, 128), jnp.float32),
            pltpu.VMEM((14, 8, 128), jnp.float32),
            dma((8,)),
            dma((16,)),
            dma((4,)),
            dma((4,)),
            dma((14,)),
            dma((5,)),
            dma((6,)),
            dma((3,)),
            dma((6,)),
            dma((4,)),
            dma((16,)),
            dma((4,)),
            dma((14,)),
            dma,
        ],
        compiler_params=pltpu.CompilerParams(
            collective_id=0, has_side_effects=True, vmem_limit_bytes=56 << 20
        ),
        cost_estimate=pl.CostEstimate(
            flops=4 * elements * head_depth, bytes_accessed=4 << 20, transcendentals=elements
        ),
    )(queries, keys, values, doc_lengths)


def token_begins(doc_starts, positions):
    hit = doc_starts[None, :] <= positions[:, None]
    return jnp.max(jnp.where(hit, doc_starts[None, :], 0), axis=1)


def absorb(
    carried, held_tiles, tile_starts, doc_starts, key_piece, value_piece, piece_start, tok_rows
):
    top_scores, denominators, runnings = carried
    piece_rows = key_piece.shape[0]
    block_width = math.gcd(piece_rows, block_keys)
    tile_count, query_rows, head_depth = held_tiles.shape
    group_size = query_rows // tok_rows
    score_scale = 1.0 / math.sqrt(head_depth)
    new_tops, new_denoms, new_runs = ([], [], [])
    for tile_num in range(tile_count):
        tile_start = tile_starts[tile_num]
        positions = tile_start + jnp.arange(tok_rows, dtype=jnp.int32)
        begins = token_begins(doc_starts, positions)
        low_pos = jnp.maximum(begins[0], piece_start)
        high_pos = jnp.minimum(tile_start + tok_rows, piece_start + piece_rows)
        first_block = low_pos // block_width
        last_block = jnp.maximum(first_block, (high_pos + block_width - 1) // block_width)
        tile_query = held_tiles[tile_num]

        def add_block(block_index, loop_state):
            top_score, denominator, running = loop_state
            offset = block_index * block_width
            key_block = lax.dynamic_slice_in_dim(key_piece, offset, block_width, 0)
            value_block = lax.dynamic_slice_in_dim(value_piece, offset, block_width, 0)
            scores = (
                lax.dot_general(
                    tile_query,
                    key_block,
                    (((1,), (1,)), ((), ())),
                    preferred_element_type=jnp.float32,
                )
                * score_scale
            )
            key_pos = offset + jnp.arange(block_width, dtype=jnp.int32)
            visible = (key_pos[None, :] <= positions[:, None]) & (
                key_pos[None, :] >= begins[:, None]
            )
            visible = jnp.repeat(visible, group_size, axis=0)
            new_top = jnp.maximum(top_score, jnp.max(jnp.where(visible, scores, neg_big), axis=1))
            weights = jnp.where(visible, jnp.exp(scores - new_top[:, None]), 0.0)
            rescale = jnp.exp(top_score - new_top)
            denominator = denominator * rescale + jnp.sum(weights, axis=1)
            running = running * rescale[:, None] + jnp.dot(
                weights.astype(jnp.bfloat16), value_block, preferred_element_type=jnp.float32
            )
            return (new_top, denominator, running)

        result = lax.fori_loop(
            first_block,
            last_block,
            add_block,
            (top_scores[tile_num], denominators[tile_num], runnings[tile_num]),
        )
        new_tops.append(result[0])
        new_denoms.append(result[1])
        new_runs.append(result[2])
    return (jnp.stack(new_tops), jnp.stack(new_denoms), jnp.stack(new_runs))


def from_all(piece):
    copies = jnp.tile(piece, (lax.axis_size("ctx"), 1))
    return lax.all_to_all(copies, "ctx", split_axis=0, concat_axis=0, tiled=True)


def any_size(queries, keys, values, doc_lengths):
    by_head = lax.all_to_all(queries, "head", split_axis=1, concat_axis=0, tiled=True)
    tok_dev = by_head.shape[0]
    head_depth = keys.shape[1]
    group_size = by_head.shape[1] // head_depth
    tile_count = 8
    tok_rows = tok_dev // tile_count
    shard_index = lax.axis_index("ctx")
    doc_starts = jnp.cumsum(doc_lengths) - doc_lengths
    tile_query = by_head.reshape(tile_count, tok_rows * group_size, head_depth)
    tile_starts = shard_index * tok_dev + jnp.arange(tile_count, dtype=jnp.int32) * tok_rows
    query_rows = tok_rows * group_size
    initial = (
        jnp.full((tile_count, query_rows), neg_big, jnp.float32),
        jnp.zeros((tile_count, query_rows), jnp.float32),
        jnp.zeros((tile_count, query_rows, head_depth), jnp.float32),
    )
    whole_keys, whole_values = (
        from_all(keys),
        from_all(values),
    )
    carried = absorb(
        initial,
        tile_query,
        tile_starts,
        doc_starts,
        whole_keys,
        whole_values,
        jnp.int32(0),
        tok_rows,
    )
    results = (carried[2] / carried[1][..., None]).astype(jnp.bfloat16)
    merged = results.reshape(tok_dev, group_size * head_depth)
    return lax.all_to_all(merged, "head", split_axis=0, concat_axis=1, tiled=True)


def per_device(queries, keys, values, doc_lengths):
    out, bound = attend(queries, keys, values, doc_lengths)
    return lax.cond(
        bound[0] <= (safe_exponent / exponent_scale) ** 2,
        lambda *_: out,
        any_size,
        queries,
        keys,
        values,
        doc_lengths,
    )


def solution(mesh):
    in_specs = (P(("ctx", "head"), None), P("ctx", "head"), P("ctx", "head"), P())
    out_specs = P(("ctx", "head"), None)
    return jax.shard_map(
        per_device, mesh=mesh, in_specs=in_specs, out_specs=out_specs, check_vma=False
    )
```
